512 devices in a mesh: gx: 32 (over z, core), gy: 16 (over x, y).
Axes of the slice: x: 4, y: 4, z: 16, core: 2. Of those that a mesh axis runs over, the one named last changes fastest.
Arguments:
- bin_resid: float32 [524288], P(('gx', 'gy')), may hold values from -0.3 to 0.3
- geometry: float32 [6, 524288], P(None, ('gx', 'gy')), may hold values from -6 to 6
- beam_weight: float32 [16, 524288], P(None, ('gx', 'gy')), may hold values from 0.05 to 1
- dest_device: int32 [524288, 1], P(('gx', 'gy')), may hold values from 0 to 511; in each aligned block of 1024 rows (0 to 1023, 1024 to 2047, ...) at most 4 rows name the same one
- dest_column: int32 [524288], P(('gx', 'gy')), may hold values from 0 to 4095
- live_count: int32 [512], P(('gx', 'gy')), may hold values from 256 to 1024, as said below
- field_sigma: float32 [6, 16], replicated, may hold values from 0.5 to 2
- x_gap: float32 [1024], replicated, may hold values from 0.00625 to 0.0625
- y_gap: float32 [2048], replicated, may hold values from 0.0015625 to 0.015625
Outputs:
- gradient: float32 [6, 16, 1024, 2048], P(None, None, 'gx', 'gy')
The draws below stay inside these ranges and needn't reach their ends.
Inputs may be any that keep to these rules, and one draw needn't show every extreme that they name: `dest_device`: within each device's block of 1024 bins no device is named more than 4 times, and some device is named exactly 4 times. `live_count`: some device has all 1024 bins live.
All inputs are finite; a program needn't handle non-finite values.
Results may differ from the reference program's by a relative error of at most 0.000094.
Values sent between devices are 32-bit elements; how exact they have to be, the bound alone decides.
No kernel may reach another device: no remote copies, remote signals or barrier semaphores. Data moves between devices by JAX's collectives and lax.ppermute only.
A program may use at most 64 MiB of HBM per device.

```python
import math
import jax
import jax.numpy as jnp
import numpy as np
from jax import lax

F = 6
LEV = 16
CX = 32
CY = 128
BINS_DEV = 1024
CAP = 4
NX = 1024
NY = 2048
N_BINS = 524288
N_GX = 32
N_GY = 16


def draw_live_count(key, part):
    key = jax.random.fold_in(key, 7)
    first_key, second_key = jax.random.split(key)
    device_count = N_GX * N_GY
    counts = jax.random.randint(first_key, (device_count,), BINS_DEV // 4, BINS_DEV + 1)
    chosen = jax.random.randint(second_key, (), 0, device_count)
    return counts.at[chosen].set(BINS_DEV).astype(jnp.int32)


def place_ends(result, stream_key, smallest, high):
    index_at = [jax.random.randint(jax.random.fold_in(stream_key, axis), (), 0, length) for axis, length in enumerate(result.shape)]
    longest = result.shape.index(max(result.shape))
    beside = index_at[:longest] + [(index_at[longest] + 1) % result.shape[longest]] + index_at[longest + 1:]
    return result.at[tuple(index_at)].set(smallest).at[tuple(beside)].set(high)


def steps_of(stream_key, shape, cuts, smallest, largest):
    factor_of, own = 1.0, jax.random.fold_in(stream_key, 6)
    for dim, shards_of in cuts:
        heights = jnp.exp(jax.random.uniform(jax.random.fold_in(own, dim), (shards_of,), jnp.float32, smallest / len(cuts), largest / len(cuts)))
        factor_of = factor_of * jnp.repeat(heights, shape[dim] // shards_of).reshape([-1 if axis == dim else 1 for axis in range(len(shape))])
    return factor_of


def shared_out(key, own, number, rows, count, top, most, skew):
    order = jax.random.permutation(key, count)
    packed, ordinary = shares(count, rows * top, most, skew, True), shares(count, rows * top, most, skew, False)
    places = jnp.arange(count)

    def named(tallies, turn):
        used = int((tallies > 0).sum())
        fixed = max(1, used // 4)
        moved = fixed + (places - fixed + turn * (used - fixed)) % max(1, count - fixed)
        return jnp.zeros((count,), jnp.int32).at[order[jnp.where(places < fixed, places, moved)]].set(jnp.asarray(tallies, jnp.int32))

    tallies = jnp.where(number % 4 == 0, named(packed, number // 4), named(ordinary, number - number // 4 - 1))
    mixed = jax.random.permutation(jax.random.fold_in(own, 3), count)
    donor, taker = mixed[0:count // 2 * 2:2], mixed[1:count // 2 * 2:2]
    slack = jnp.minimum(tallies[donor] - 1, most - tallies[taker]) // 2
    slack = jnp.where((donor == order[0]) | (taker == order[0]) | (tallies[taker] == 0), 0, jnp.maximum(slack, 0))
    moved = jax.random.randint(jax.random.fold_in(own, 4), (count // 2,), 0, 1 << 20) % (slack + 1)
    tallies = tallies.at[donor].add(-moved).at[taker].add(moved)
    items = jnp.searchsorted(jnp.cumsum(tallies), jnp.arange(rows * top), side="right").astype(jnp.int32)
    table = items.reshape(top, rows).T
    table = table[jax.random.permutation(jax.random.fold_in(own, 1), rows)]
    turn = jax.random.randint(jax.random.fold_in(own, 2), (rows, 1), 0, top)
    return jnp.take_along_axis(table, (jnp.arange(top)[None, :] + turn) % top, axis=1)


def shares(count, total, reach, slope, full):
    weights = [(1 << 20) // math.isqrt(grade ** slope) + 1 for grade in range(1, count + 1)]
    largest = reach if full else min(reach, max(-(-total // count), total * weights[0] // sum(weights)))
    least = 1 if total - largest >= count - 1 else 0
    holding, spare = [largest] + [least] * (count - 1), total - largest - least * (count - 1)
    while spare > 0:
        free = [i for i in range(1, count) if holding[i] < largest] or [i for i in range(1, count) if holding[i] < reach]
        whole, budget = sum([weights[i] for i in free]), spare
        for i in free:
            more = min(reach - holding[i], max(1, budget * weights[i] // whole), spare)
            holding[i] = holding[i] + more
            spare = spare - more
    return np.array(holding)


def normal_values(own_key, shape, width, most, pieces=(), held_as=jnp.bfloat16):
    values = width * jax.random.normal(own_key, shape, jnp.float32)
    if pieces:
        values = values * steps_of(own_key, shape, pieces, -0.22, 0.18)
    return jnp.clip(values, -most, most).astype(held_as)


def setup_inputs(seed: int = 0) -> dict:
    seeds = jax.random.split(jax.random.key(seed), 10)
    bin_resid = normal_values(seeds[0], (N_BINS,), 0.05, 0.3, ((0, 512),), jnp.float32)
    geometry = normal_values(seeds[1], (F, N_BINS), 1.0, 6.0, ((1, 512),), jnp.float32)
    beam_weight = jnp.clip(0.05 + 0.95 * jax.random.uniform(seeds[2], (LEV, N_BINS), jnp.float32) ** steps_of(seeds[2], (LEV, N_BINS), ((1, 512),), -0.2, 0.2), 0.05, 1.0)
    dest_device_keys = jax.random.split(jax.random.fold_in(seeds[3], 1), N_BINS // BINS_DEV)
    dest_device_turns = jax.random.permutation(jax.random.fold_in(seeds[3], 3), N_BINS // BINS_DEV)
    dest_device = jax.vmap(lambda own, number: shared_out(jax.random.fold_in(seeds[3], 2), own, number, BINS_DEV, N_GX * N_GY, 1, CAP, 2))(dest_device_keys, dest_device_turns).reshape((N_BINS, 1))
    dest_column = place_ends(jax.random.randint(seeds[4], (N_BINS,), 0, CX * CY), jax.random.fold_in(seeds[4], 1), 0, (CX * CY) - 1).astype(jnp.int32)
    live_count = draw_live_count(jax.random.fold_in(seeds[9], 71), 0)
    field_sigma = jnp.clip(jnp.exp(jax.random.uniform(seeds[6], (F, LEV), jnp.float32, math.log(0.5), math.log(2.0))), 0.5, 2.0)
    x_gap = jnp.clip(jnp.exp(jax.random.uniform(seeds[7], (NX,), jnp.float32, math.log(0.00625), math.log(0.0625))), 0.00625, 0.0625)
    y_gap = jnp.clip(jnp.exp(jax.random.uniform(seeds[8], (NY,), jnp.float32, math.log(0.0015625), math.log(0.015625))), 0.0015625, 0.015625)
    return dict(bin_resid=bin_resid, geometry=geometry, beam_weight=beam_weight, dest_device=dest_device, dest_column=dest_column, live_count=live_count, field_sigma=field_sigma, x_gap=x_gap, y_gap=y_gap)


def one_pass(line_vals, coefficient, backward):

    def step_fn(carried, step_in):
        point, factor = step_in
        carried = point + factor * carried
        return (carried, carried)
    _, passed = lax.scan(step_fn, jnp.zeros_like(line_vals[0]), (line_vals, coefficient), reverse=backward)
    return passed

def line_smooth(line_vals, gap_vals):
    decay_coef = 1.0 - gap_vals
    scale_coef = jnp.sqrt(gap_vals * (2.0 - gap_vals))[:, None, None]
    padding = jnp.zeros((1,), jnp.float32)
    prior_coef = jnp.concatenate([padding, decay_coef[:-1]])
    later_coef = jnp.concatenate([decay_coef[1:], padding])
    fore_pass = one_pass(line_vals, prior_coef, False) * scale_coef
    return one_pass(fore_pass, later_coef, True) * scale_coef

def reference(bin_resid, geometry, beam_weight, dest_device, dest_column, live_count, field_sigma, x_gap, y_gap):
    bin_count = bin_resid.shape[0]
    bin_index = jnp.arange(bin_count, dtype=jnp.int32)
    owner_dev = bin_index // BINS_DEV
    alive_mask = (bin_index % BINS_DEV < live_count[owner_dev]).astype(jnp.float32)
    weighted = geometry * (alive_mask * bin_resid)[None, :]
    dest_dev = dest_device[:, 0]
    cell_x = dest_dev // N_GY * CX + dest_column // CY
    cell_y = dest_dev % N_GY * CY + dest_column % CY
    cell_flat = (cell_x * NY + cell_y).astype(jnp.int32)
    outer_prod = (weighted[:, None, :] * beam_weight[None, :, :]).reshape(F * LEV, bin_count).T
    summed = jax.ops.segment_sum(outer_prod, cell_flat, num_segments=NX * NY)
    adjoint = summed.T.reshape(F, LEV, NX, NY)
    scaled = adjoint * field_sigma[:, :, None, None]

    def filter_field(field_vals):
        along_x = jnp.moveaxis(field_vals, 1, 0)
        along_x = jnp.moveaxis(line_smooth(along_x, x_gap), 0, 1)
        along_y = jnp.moveaxis(along_x, 2, 0)
        return jnp.moveaxis(line_smooth(along_y, y_gap), 0, 2)
    return lax.map(filter_field, scaled)
```

```python
import functools
import jax
import jax.numpy as jnp
from jax import lax
from jax.experimental import pallas as pl
from jax.experimental.pallas import tpu as pltpu
from jax.sharding import PartitionSpec as P

F32 = jnp.float32
BF16 = jnp.bfloat16
I32 = jnp.int32
LANES = 128
FIELDS = 6
LEVELS = 16
DEPTH = FIELDS * LEVELS
SLOTS = 4
WIDTH = 32
CX = 32
CY = 128
NEAR = 4

params = functools.partial(pltpu.CompilerParams, vmem_limit_bytes=48 * 1024 * 1024)
vmem = pl.BlockSpec(memory_space=pltpu.VMEM)
smem = pl.BlockSpec(memory_space=pltpu.SMEM)


def iota(shape, dim):
    return lax.broadcasted_iota(I32, shape, dim)


def split_two(values):
    high = values.astype(BF16)
    return high, (values - high.astype(F32)).astype(BF16)


def dot_nt(left, right):
    return lax.dot_general(left, right, (((1,), (1,)), ((), ())), preferred_element_type=F32)


def dot_nn(left, right):
    return lax.dot_general(left, right, (((1,), (0,)), ((), ())), preferred_element_type=F32)


def pack_kernel(live_ref, resid_ref, dest_ref, column_ref, geometry_ref, beam_ref, send_ref):
    bins = resid_ref.shape[1]
    peers = send_ref.shape[0]
    dest = dest_ref[...]
    dest_f = dest.astype(F32)
    dest_t = jnp.broadcast_to(dest_f, (LANES, bins)).T
    ranks = []
    for chunk in range(bins // LANES):
        rows = (chunk + 1) * LANES
        same = dest_t[:rows] == dest_f[:, chunk * LANES : rows]
        before = iota((rows, LANES), 0) < iota((rows, LANES), 1) + chunk * LANES
        ranks.append(jnp.sum(jnp.where(same & before, 1.0, 0.0), axis=0, keepdims=True))
    rank = jnp.concatenate(ranks, axis=1)
    alive = jnp.where(iota((1, bins), 1) < live_ref[0], 1.0, 0.0)
    weighted = geometry_ref[...] * (alive * resid_ref[...])
    payload = jnp.concatenate(
        [
            beam_ref[...],
            weighted,
            column_ref[...].astype(F32),
            jnp.zeros((WIDTH - LEVELS - FIELDS - 1, bins), F32),
        ],
        axis=0,
    )
    spread = jnp.concatenate([jnp.where(rank == float(s), payload, 0.0) for s in range(SLOTS)], axis=0)
    high = spread.astype(BF16)
    rest = spread - high.astype(F32)
    middle = rest.astype(BF16)
    low = (rest - middle.astype(F32)).astype(BF16)
    onehot = jnp.where(iota((peers, bins), 0) == dest, 1.0, 0.0).astype(BF16)
    send_ref[...] = dot_nt(onehot, high) + (dot_nt(onehot, middle) + dot_nt(onehot, low))


def coef_kernel(y_flat, x_cols, y_cols, y_rows, dt_high, dt_low, edge_ref, block_ref, chain, alphas):
    own = lax.axis_index("gy")
    length = y_rows.shape[1] * LANES

    def block_scalars(cols, row):
        steps, blocks = cols.shape[1:]

        def forward(p, value):
            value = value * cols[0, pl.ds(p, 1), :]
            alphas[pl.ds(p, 1), :blocks] = value
            return value

        alpha = lax.fori_loop(0, steps, forward, jnp.ones((1, blocks), F32))

        def backward(k, carried):
            gamma, beta = carried
            p = steps - 1 - k
            later = cols[1, pl.ds(p, 1), :]
            gamma = cols[2, pl.ds(p, 1), :] * alphas[pl.ds(p, 1), :blocks] + later * gamma
            return gamma, beta * later

        gamma, beta = lax.fori_loop(
            0, steps, backward, (jnp.zeros((1, blocks), F32), jnp.ones((1, blocks), F32))
        )
        block_ref[row : row + 1, :blocks] = alpha
        block_ref[row + 1 : row + 2, :blocks] = beta
        block_ref[row + 2 : row + 3, :blocks] = gamma

    block_ref[...] = jnp.zeros(block_ref.shape, F32)
    block_scalars(x_cols, 0)
    block_scalars(y_cols, 3)

    first = own * CY
    lane = iota((1, LANES), 1)

    def fill(n, row):
        row = jnp.where(lane == n, 1.0, row * y_flat[first + n])
        chain[pl.ds(n, 1), :] = row
        return row

    lax.fori_loop(0, CY, fill, jnp.zeros((1, LANES), F32))

    def unfill(k, row):
        n = CY - 1 - k
        row = chain[pl.ds(n, 1), :] * y_flat[2 * length + first + n] + row * y_flat[length + first + n]
        chain[pl.ds(n, 1), :] = row
        return row

    lax.fori_loop(0, CY, unfill, jnp.zeros((1, LANES), F32))
    scale = y_rows[2, pl.ds(own, 1), :]
    filt = chain[...].T * scale
    high, low = split_two(filt)
    dt_high[...] = high
    dt_low[...] = low
    scale_first = jnp.broadcast_to(scale[:, :1], (1, LANES))
    scale_last = jnp.broadcast_to(scale[:, CY - 1 :], (1, LANES))
    edge_ref[...] = jnp.zeros(edge_ref.shape, F32)
    edge_ref[0:1] = filt[:1] * y_flat[first]
    edge_ref[1:2] = filt[CY - 1 :] * y_flat[length + first + CY - 1] / scale_last
    edge_ref[2:3] = 1.0 / jnp.where(lane % 64 < CX, scale_last * scale_last, scale_first)


def grid_kernel(recv_ref, sigma_ref, dt_high, dt_low, edge_ref, block_out, ends_out, outer, column):
    sources = recv_ref.shape[0]
    turned = recv_ref[...].T
    for s in range(SLOTS):
        at = slice(s * sources, (s + 1) * sources)
        base = s * WIDTH
        beam = turned[base : base + LEVELS]
        for f in range(FIELDS):
            weight = turned[base + LEVELS + f : base + LEVELS + f + 1]
            high, low = split_two(beam * weight)
            outer[f * LEVELS : (f + 1) * LEVELS, at] = high
            outer[DEPTH + f * LEVELS : DEPTH + (f + 1) * LEVELS, at] = low
        place = base + LEVELS + FIELDS
        column[at, :] = jnp.broadcast_to(recv_ref[:, place : place + 1], (sources, LANES))
    lane_f = iota((1, LANES), 1).astype(F32)
    lane = iota((DEPTH, LANES), 1)
    sigma = sigma_ref[...]

    def step(n, ends):
        cols = column[...]
        start = (n * (2 * CY)).astype(F32)
        hit = [jnp.where(cols == lane_f + (start + h * CY), 1.0, 0.0).astype(BF16) for h in range(2)]
        summed = dot_nn(outer[...], jnp.concatenate(hit, axis=1))
        summed = summed[:DEPTH] + summed[DEPTH:]
        scaled = jnp.concatenate([summed[:, :CY] * sigma, summed[:, CY:] * sigma], axis=0)
        high, low = split_two(scaled)
        passed = dot_nn(high, dt_high[...]) + (dot_nn(low, dt_high[...]) + dot_nn(high, dt_low[...]))
        for h in range(2):
            part = passed[h * DEPTH : (h + 1) * DEPTH]
            x = 2 * n + h
            block_out[x] = part
            ends = jnp.where(lane == x, part[:, CY - 1 :], ends)
            ends = jnp.where(lane == x + CX, part[:, :1], ends)
        return ends

    ends = lax.fori_loop(0, CX // 2, step, jnp.zeros((DEPTH, LANES), F32))
    half = DEPTH // 2
    both = jnp.where(iota((half, LANES), 1) < 64, ends[:half], pltpu.roll(ends[half:], 64, 1))
    both = both * edge_ref[2:3]
    for j in range(ends_out.shape[0]):
        ends_out[j] = both


def line_kernel(block_tab, x_flat, ends_ref, edge_ref, block_ref, block_out, sums_out):
    own_y = lax.axis_index("gy")
    first = lax.axis_index("gx") * CX
    length = x_flat.shape[0] // 3
    count, half, _ = ends_ref.shape
    zero = jnp.zeros((half, LANES), F32)
    fore, fore_own, fores = zero, zero, []
    for j in range(count):
        fores.append(fore)
        fore_own = jnp.where(own_y == j, fore, fore_own)
        fore = ends_ref[j] + block_tab[3, j] * fore
    back, back_own = zero, zero
    for j in reversed(range(count)):
        back_own = jnp.where(own_y == j, back, back_own)
        back = ends_ref[j] + block_tab[5, j] * pltpu.roll(fores[j], CX, 1) + block_tab[4, j] * back
    both = jnp.where(iota((half, LANES), 1) % 64 < CX, fore_own, back_own)
    both = jnp.concatenate([both, pltpu.roll(both, 64, 1)], axis=0)
    edge_fore = edge_ref[0:1]
    edge_back = edge_ref[1:2]
    run = jnp.zeros((DEPTH, LANES), F32)
    begin = jnp.zeros((DEPTH, LANES), F32)
    weight = jnp.float32(1.0)
    for x in range(CX):
        part = block_ref[x] + both[:, x : x + 1] * edge_fore + both[:, CX + x : CX + x + 1] * edge_back
        block_out[x] = part
        run = part if x == 0 else part + x_flat[first + x] * run
        begin = begin + (weight * x_flat[2 * length + first + x]) * run
        weight = weight * x_flat[length + first + x]
    rows = DEPTH // NEAR
    for k in range(NEAR):
        sums_out[k, :rows] = run[k * rows : (k + 1) * rows]
        sums_out[k, rows:] = begin[k * rows : (k + 1) * rows]


def join_kernel(block_tab, sums_ref, joined_out):
    start = lax.axis_index("gx") // NEAR * NEAR
    rows = sums_ref.shape[1] // 2
    fore = jnp.zeros((rows, LANES), F32)
    fores = []
    for k in range(NEAR):
        fores.append(fore)
        fore = sums_ref[k, :rows] + block_tab[0, start + k] * fore
    back = jnp.zeros((rows, LANES), F32)
    for k in reversed(range(NEAR)):
        back = (
            sums_ref[k, rows:]
            + block_tab[2, start + k] * fores[k]
            + block_tab[1, start + k] * back
        )
    for g in range(joined_out.shape[0]):
        joined_out[g, :rows] = fore
        joined_out[g, rows:] = back


def carry_kernel(block_tab, joined_ref, sums_ref, carry_out):
    own = lax.axis_index("gx") // NEAR
    start = own * NEAR
    groups = joined_ref.shape[0]
    rows = sums_ref.shape[1] // 2
    zero = jnp.zeros((rows, LANES), F32)
    fore, fore_own, fores, betas, gammas = zero, zero, [], [], []
    for g in range(groups):
        entries = [jnp.float32(1.0)]
        for k in range(NEAR):
            entries.append(entries[-1] * block_tab[0, g * NEAR + k])
        gamma, beta = jnp.float32(0.0), jnp.float32(1.0)
        for k in reversed(range(NEAR)):
            b = block_tab[1, g * NEAR + k]
            gamma = block_tab[2, g * NEAR + k] * entries[k] + b * gamma
            beta = beta * b
        gammas.append(gamma)
        betas.append(beta)
        fores.append(fore)
        fore_own = jnp.where(own == g, fore, fore_own)
        fore = joined_ref[g, :rows] + entries[NEAR] * fore
    back, back_own = zero, zero
    for g in reversed(range(groups)):
        back_own = jnp.where(own == g, back, back_own)
        back = joined_ref[g, rows:] + gammas[g] * fores[g] + betas[g] * back
    fore, back, fores = fore_own, back_own, []
    for k in range(NEAR):
        carry_out[k, :rows] = fore
        fores.append(fore)
        fore = sums_ref[k, :rows] + block_tab[0, start + k] * fore
    for k in reversed(range(NEAR)):
        carry_out[k, rows:] = back
        back = (
            sums_ref[k, rows:]
            + block_tab[2, start + k] * fores[k]
            + block_tab[1, start + k] * back
        )


def final_kernel(x_flat, carry_ref, block_ref, out_ref, scaled):
    first = lax.axis_index("gx") * CX
    length = x_flat.shape[0] // 3
    rows = carry_ref.shape[1] // 2
    run = jnp.concatenate([carry_ref[k, :rows] for k in range(NEAR)], axis=0)
    back = jnp.concatenate([carry_ref[k, rows:] for k in range(NEAR)], axis=0)
    for x in range(CX):
        run = block_ref[x] + x_flat[first + x] * run
        scaled[x] = x_flat[2 * length + first + x] * run
    for x in reversed(range(CX)):
        back = scaled[x] + x_flat[length + first + x] * back
        out_ref[pl.ds(x, DEPTH, stride=CX), :] = x_flat[2 * length + first + x] * back


def table(gap):
    decay = 1.0 - gap
    edge = jnp.zeros((1,), F32)
    prior = jnp.concatenate([edge, decay[:-1]])
    later = jnp.concatenate([decay[1:], edge])
    return jnp.stack([prior, later, jnp.sqrt(gap * (2.0 - gap))])


def call(kernel, outs, specs, scratch=()):
    shapes = tuple(jax.ShapeDtypeStruct(s, t) for s, t in outs)
    return pl.pallas_call(
        kernel,
        out_shape=shapes if len(shapes) > 1 else shapes[0],
        in_specs=specs,
        out_specs=(vmem,) * len(shapes) if len(shapes) > 1 else vmem,
        scratch_shapes=scratch,
        compiler_params=params(),
    )


def local(bin_resid, geometry, beam_weight, dest_device, dest_column, live_count, field_sigma, x_gap, y_gap):
    count_x = lax.axis_size("gx")
    count_y = lax.axis_size("gy")
    peers = count_x * count_y
    bins = bin_resid.shape[0]
    far = count_x // NEAR
    near_groups = [[g * NEAR + k for k in range(NEAR)] for g in range(far)]
    far_groups = [[g * NEAR + k for g in range(far)] for k in range(NEAR)]
    a2a = functools.partial(lax.all_to_all, tiled=True)

    send = call(pack_kernel, [((peers, LANES), F32)], [smem] + [vmem] * 5)(
        live_count,
        bin_resid.reshape(1, bins),
        dest_device.reshape(1, bins),
        dest_column.reshape(1, bins),
        geometry,
        beam_weight,
    )
    tab_x = table(x_gap)
    tab_y = table(y_gap)
    x_flat = tab_x.reshape(-1)
    dt_high, dt_low, edge, blocks = call(
        coef_kernel,
        [((CY, CY), BF16), ((CY, CY), BF16), ((8, LANES), F32), ((8, LANES), F32)],
        [smem, vmem, vmem, vmem],
        [pltpu.VMEM((CY, LANES), F32), pltpu.VMEM((CY, LANES), F32)],
    )(
        tab_y.reshape(-1),
        tab_x.reshape(3, count_x, CX).transpose(0, 2, 1),
        tab_y.reshape(3, count_y, CY).transpose(0, 2, 1),
        tab_y.reshape(3, count_y, CY),
    )
    sigma = jnp.broadcast_to(field_sigma.reshape(DEPTH, 1), (DEPTH, LANES))

    moved = a2a(send.reshape(count_x, count_y, LANES), "gx", split_axis=0, concat_axis=0)
    moved = a2a(moved, "gy", split_axis=1, concat_axis=1)
    block, ends = call(
        grid_kernel,
        [((CX, DEPTH, LANES), F32), ((count_y, DEPTH // 2, LANES), F32)],
        [vmem] * 5,
        [pltpu.VMEM((2 * DEPTH, SLOTS * peers), BF16), pltpu.VMEM((SLOTS * peers, LANES), F32)],
    )(moved.reshape(peers, LANES), sigma, dt_high, dt_low, edge)
    ends = a2a(ends, "gy", split_axis=0, concat_axis=0)
    block, sums = call(
        line_kernel,
        [((CX, DEPTH, LANES), F32), ((NEAR, 2 * DEPTH // NEAR, LANES), F32)],
        [smem, smem, vmem, vmem, vmem],
    )(blocks, x_flat, ends, edge, block)
    sums = a2a(sums, "gx", split_axis=0, concat_axis=0, axis_index_groups=near_groups)
    joined = call(join_kernel, [((far, 2 * DEPTH // NEAR, LANES), F32)], [smem, vmem])(blocks, sums)
    joined = a2a(joined, "gx", split_axis=0, concat_axis=0, axis_index_groups=far_groups)
    carry = call(carry_kernel, [((NEAR, 2 * DEPTH // NEAR, LANES), F32)], [smem, vmem, vmem])(
        blocks, joined, sums
    )
    carry = a2a(carry, "gx", split_axis=0, concat_axis=0, axis_index_groups=near_groups)
    out = call(
        final_kernel,
        [((DEPTH * CX, LANES), F32)],
        [smem, vmem, vmem],
        [pltpu.VMEM((CX, DEPTH, LANES), F32)],
    )(x_flat, carry, block)
    return out.reshape(FIELDS, LEVELS, CX, CY)


def solution(mesh):
    both = ("gx", "gy")
    placed = (P(both), P(None, both), P(None, both), P(both, None), P(both), P(both), P(), P(), P())
    return jax.shard_map(
        local, mesh=mesh, in_specs=placed, out_specs=P(None, None, "gx", "gy"), check_vma=False
    )
```

```python
import functools
import jax
import jax.numpy as jnp
from jax import lax
from jax.experimental import pallas as pl
from jax.experimental.pallas import tpu as pltpu
from jax.sharding import PartitionSpec as P

F32 = jnp.float32
BF16 = jnp.bfloat16
I32 = jnp.int32
LANES = 128
FIELDS = 6
LEVELS = 16
DEPTH = FIELDS * LEVELS
SLOTS = 4
WIDTH = 32
CX = 32
CY = 128
NEAR = 4

params = functools.partial(pltpu.CompilerParams, vmem_limit_bytes=48 * 1024 * 1024)
vmem = pl.BlockSpec(memory_space=pltpu.VMEM)
smem = pl.BlockSpec(memory_space=pltpu.SMEM)


def iota(shape, dim):
    return lax.broadcasted_iota(I32, shape, dim)


def split_two(values):
    high = values.astype(BF16)
    return high, (values - high.astype(F32)).astype(BF16)


def dot_nt(left, right):
    return lax.dot_general(left, right, (((1,), (1,)), ((), ())), preferred_element_type=F32)


def dot_nn(left, right):
    return lax.dot_general(left, right, (((1,), (0,)), ((), ())), preferred_element_type=F32)


def pack_kernel(live_ref, resid_ref, dest_ref, column_ref, geometry_ref, beam_ref, send_ref):
    bins = resid_ref.shape[1]
    peers = send_ref.shape[0]
    dest = dest_ref[...]
    dest_f = dest.astype(F32)
    dest_t = jnp.broadcast_to(dest_f, (LANES, bins)).T
    ranks = []
    for chunk in range(bins // LANES):
        rows = (chunk + 1) * LANES
        same = dest_t[:rows] == dest_f[:, chunk * LANES : rows]
        before = iota((rows, LANES), 0) < iota((rows, LANES), 1) + chunk * LANES
        ranks.append(jnp.sum(jnp.where(same & before, 1.0, 0.0), axis=0, keepdims=True))
    rank = jnp.concatenate(ranks, axis=1)
    alive = jnp.where(iota((1, bins), 1) < live_ref[0], 1.0, 0.0)
    weighted = geometry_ref[...] * (alive * resid_ref[...])
    payload = jnp.concatenate(
        [
            beam_ref[...],
            weighted,
            column_ref[...].astype(F32),
            jnp.zeros((WIDTH - LEVELS - FIELDS - 1, bins), F32),
        ],
        axis=0,
    )
    spread = jnp.concatenate([jnp.where(rank == float(s), payload, 0.0) for s in range(SLOTS)], axis=0)
    high = spread.astype(BF16)
    rest = spread - high.astype(F32)
    middle = rest.astype(BF16)
    low = (rest - middle.astype(F32)).astype(BF16)
    onehot = jnp.where(iota((peers, bins), 0) == dest, 1.0, 0.0).astype(BF16)
    send_ref[...] = dot_nt(onehot, high) + (dot_nt(onehot, middle) + dot_nt(onehot, low))


def coef_kernel(x_flat, y_flat, x_cols, y_cols, y_rows, dt_high, dt_low, tab_ref, edge_ref, block_ref, ends_ref, chain, gammas, betas):
    own_x = lax.axis_index("gx")
    own_y = lax.axis_index("gy")
    length = y_rows.shape[1] * LANES
    span = x_cols.shape[2] * CX

    def block_scalars(cols, row):
        steps, blocks = cols.shape[1:]

        def forward(p, value):
            value = value * cols[0, pl.ds(p, 1), :]
            gammas[pl.ds(p, 1), :blocks] = value
            return value

        alpha = lax.fori_loop(0, steps, forward, jnp.ones((1, blocks), F32))

        def backward(k, carried):
            gamma, beta = carried
            p = steps - 1 - k
            later = cols[1, pl.ds(p, 1), :]
            gamma = cols[2, pl.ds(p, 1), :] * gammas[pl.ds(p, 1), :blocks] + later * gamma
            beta = beta * later
            gammas[pl.ds(p, 1), :blocks] = gamma
            betas[pl.ds(p, 1), :blocks] = beta
            return gamma, beta

        gamma, beta = lax.fori_loop(
            0, steps, backward, (jnp.zeros((1, blocks), F32), jnp.ones((1, blocks), F32))
        )
        block_ref[row : row + 1, :blocks] = alpha
        block_ref[row + 1 : row + 2, :blocks] = beta
        block_ref[row + 2 : row + 3, :blocks] = gamma

    block_ref[...] = jnp.zeros(block_ref.shape, F32)
    block_scalars(y_cols, 3)
    block_scalars(x_cols, 0)
    blocks = x_cols.shape[2]
    mine = iota((CX, blocks), 1) == own_x
    for k, scratch in enumerate((gammas, betas)):
        picked = jnp.where(mine, scratch[:CX, :blocks] * x_cols[2], 0.0)
        ends_ref[k * CX : (k + 1) * CX] = jnp.broadcast_to(
            jnp.sum(picked, axis=1, keepdims=True), (CX, LANES)
        )

    lane = iota((1, LANES), 1)
    first = own_x * CX
    down = []
    weight = jnp.float32(1.0)
    for x in range(CX):
        down.append(weight * x_flat[2 * span + first + x])
        weight = weight * x_flat[span + first + x]
    tail, start = jnp.float32(1.0), down[CX - 1]
    tails, starts = [tail], [start]
    for x in reversed(range(CX - 1)):
        factor = x_flat[first + x + 1]
        tail = tail * factor
        start = down[x] + factor * start
        tails.append(tail)
        starts.append(start)
    row_tail = jnp.zeros((1, LANES), F32)
    row_start = jnp.zeros((1, LANES), F32)
    for x in range(CX):
        row_tail = jnp.where(lane % CX == x, tails[CX - 1 - x], row_tail)
        row_start = jnp.where(lane % CX == x, starts[CX - 1 - x], row_start)

    first = own_y * CY

    def fill(n, row):
        row = jnp.where(lane == n, 1.0, row * y_flat[first + n])
        chain[pl.ds(n, 1), :] = row
        return row

    lax.fori_loop(0, CY, fill, jnp.zeros((1, LANES), F32))

    def unfill(k, row):
        n = CY - 1 - k
        row = chain[pl.ds(n, 1), :] * y_flat[2 * length + first + n] + row * y_flat[length + first + n]
        chain[pl.ds(n, 1), :] = row
        return row

    lax.fori_loop(0, CY, unfill, jnp.zeros((1, LANES), F32))
    scale = y_rows[2, pl.ds(own_y, 1), :]
    filt = chain[...].T * scale
    high, low = split_two(filt)
    dt_high[...] = high
    dt_low[...] = low
    scale_first = scale[:, :1]
    scale_last = scale[:, CY - 1 :]
    tab_ref[0] = jnp.broadcast_to(filt[:, CY - 1 :] / (scale_last * scale_last), (CY, LANES))
    tab_ref[1] = jnp.broadcast_to(filt[:, :1] / scale_first, (CY, LANES))
    edge_ref[...] = jnp.zeros(edge_ref.shape, F32)
    edge_ref[0:1] = filt[:1] * y_flat[first]
    edge_ref[1:2] = filt[CY - 1 :] * y_flat[length + first + CY - 1] / scale_last
    edge_ref[2:3] = row_tail
    edge_ref[3:4] = row_start


def ends_kernel(recv_ref, sigma_ref, tab_ref, outer_out, column_out, ends_out, outer):
    sources = recv_ref.shape[0]
    turned = recv_ref[...].T
    weights = [jnp.concatenate([tab_ref[c]] * (sources // LANES), axis=1) for c in range(2)]
    hits = []
    for s in range(SLOTS):
        at = slice(s * sources, (s + 1) * sources)
        base = s * WIDTH
        beam = turned[base : base + LEVELS]
        place = turned[base + LEVELS + FIELDS : base + LEVELS + FIELDS + 1]
        column_out[:, at] = place
        place = place.astype(I32)
        on_y = iota((CY, sources), 0) == (place & (CY - 1))
        ends = [jnp.sum(jnp.where(on_y, w, 0.0), axis=0, keepdims=True) for w in weights]
        hits.append(jnp.where((iota((LANES, sources), 0) & (CX - 1)) == (place >> 7), 1.0, 0.0).astype(BF16))
        for f in range(FIELDS):
            prod = beam * turned[base + LEVELS + f : base + LEVELS + f + 1]
            rows = slice(f * LEVELS, (f + 1) * LEVELS)
            high, low = split_two(prod)
            outer_out[rows, at] = high
            outer_out[DEPTH + f * LEVELS : DEPTH + (f + 1) * LEVELS, at] = low
            for c in range(2):
                high, low = split_two(prod * ends[c])
                outer[(2 * c) * DEPTH + f * LEVELS : (2 * c) * DEPTH + (f + 1) * LEVELS, at] = high
                outer[(2 * c + 1) * DEPTH + f * LEVELS : (2 * c + 1) * DEPTH + (f + 1) * LEVELS, at] = low
    summed = dot_nt(outer[...], jnp.concatenate(hits, axis=1))
    sigma = sigma_ref[...]
    fore = (summed[:DEPTH] + summed[DEPTH : 2 * DEPTH]) * sigma
    back = (summed[2 * DEPTH : 3 * DEPTH] + summed[3 * DEPTH :]) * sigma
    half = DEPTH // 2
    lane = iota((half, LANES), 1)
    both = jnp.where(
        lane < 64,
        jnp.where(lane < 32, fore[:half], back[:half]),
        jnp.where(lane < 96, fore[half:], back[half:]),
    )
    for j in range(ends_out.shape[0]):
        ends_out[j] = both


def grid_kernel(x_flat, outer_ref, column_ref, recv_ref, sigma_ref, dt_high, dt_low, block_out, sums_out, masked, hit):
    sources = recv_ref.shape[0]
    first = lax.axis_index("gx") * CX
    length = x_flat.shape[0] // 3
    lane2 = iota((1, 2 * LANES), 1)
    for s in range(SLOTS):
        place = s * WIDTH + LEVELS + FIELDS
        cols = jnp.broadcast_to(recv_ref[:, place : place + 1], (sources, LANES)).astype(I32) & (2 * CY - 1)
        cols = jnp.concatenate([cols, cols], axis=1)
        hit[s * sources : (s + 1) * sources] = jnp.where(cols == lane2, 1.0, 0.0).astype(BF16)
    pair = column_ref[...].astype(I32) >> 8
    sigma = sigma_ref[...]
    group = 4

    def step(n, carried):
        run, begin, weight = carried
        for c in range(group):
            keep = jnp.where(pair == n * group + c, 1.0, 0.0)
            keep = jnp.broadcast_to(keep, (16, keep.shape[1])).astype(BF16)
            for r in range(2 * DEPTH // 16):
                masked[c * 2 * DEPTH + r * 16 : c * 2 * DEPTH + (r + 1) * 16] = (
                    outer_ref[r * 16 : (r + 1) * 16] * keep
                )
        summed = dot_nn(masked[...], hit[...])
        parts = []
        for c in range(group):
            both = summed[c * 2 * DEPTH : c * 2 * DEPTH + DEPTH] + summed[c * 2 * DEPTH + DEPTH : (c + 1) * 2 * DEPTH]
            parts += [both[:, :CY] * sigma, both[:, CY:] * sigma]
        high, low = split_two(jnp.concatenate(parts, axis=0))
        passed = dot_nn(high, dt_high[...]) + (dot_nn(low, dt_high[...]) + dot_nn(high, dt_low[...]))
        for h in range(2 * group):
            part = passed[h * DEPTH : (h + 1) * DEPTH]
            x = n * 2 * group + h
            block_out[x] = part
            run = part + jnp.where(x == 0, 0.0, x_flat[first + x]) * run
            begin = begin + (weight * x_flat[2 * length + first + x]) * run
            weight = weight * x_flat[length + first + x]
        return run, begin, weight

    zero = jnp.zeros((DEPTH, LANES), F32)
    run, begin, _ = lax.fori_loop(0, CX // (2 * group), step, (zero, zero, jnp.float32(1.0)))
    sums_out[0] = run
    sums_out[1] = begin


def line_kernel(block_tab, ends_ref, edge_ref, raw_ref, both_out, sums_out):
    own_y = lax.axis_index("gy")
    count, half, _ = ends_ref.shape
    zero = jnp.zeros((half, LANES), F32)
    fore, fore_own, fores = zero, zero, []
    for j in range(count):
        fores.append(fore)
        fore_own = jnp.where(own_y == j, fore, fore_own)
        fore = ends_ref[j] + block_tab[3, j] * fore
    back, back_own = zero, zero
    for j in reversed(range(count)):
        back_own = jnp.where(own_y == j, back, back_own)
        back = ends_ref[j] + block_tab[5, j] * pltpu.roll(fores[j], CX, 1) + block_tab[4, j] * back
    both = jnp.where(iota((half, LANES), 1) % 64 < CX, fore_own, back_own)
    both = jnp.concatenate([both, pltpu.roll(both, 64, 1)], axis=0)
    both_out[...] = both
    lane = iota((DEPTH, LANES), 1)
    edge_fore = edge_ref[0:1]
    edge_back = edge_ref[1:2]
    rows = DEPTH // NEAR
    for c in range(2):
        weighted = both * edge_ref[2 + c : 3 + c]
        fore_part = jnp.sum(jnp.where(lane < CX, weighted, 0.0), axis=1, keepdims=True)
        back_part = jnp.sum(jnp.where((lane >= CX) & (lane < 2 * CX), weighted, 0.0), axis=1, keepdims=True)
        total = raw_ref[c] + fore_part * edge_fore + back_part * edge_back
        for k in range(NEAR):
            sums_out[k, c * rows : (c + 1) * rows] = total[k * rows : (k + 1) * rows]


def scan_kernel(x_flat, both_ref, edge_ref, block_ref, out_ref, scaled):
    first = lax.axis_index("gx") * CX
    length = x_flat.shape[0] // 3
    both = both_ref[...]
    edge_fore = edge_ref[0:1]
    edge_back = edge_ref[1:2]
    run = jnp.zeros((DEPTH, LANES), F32)
    for x in range(CX):
        part = block_ref[x] + both[:, x : x + 1] * edge_fore + both[:, CX + x : CX + x + 1] * edge_back
        run = part if x == 0 else part + x_flat[first + x] * run
        scaled[x] = x_flat[2 * length + first + x] * run
    back = jnp.zeros((DEPTH, LANES), F32)
    for x in reversed(range(CX)):
        back = scaled[x] if x == CX - 1 else scaled[x] + x_flat[length + first + x] * back
        out_ref[pl.ds(x, DEPTH, stride=CX), :] = x_flat[2 * length + first + x] * back


def join_kernel(block_tab, sums_ref, joined_out):
    start = lax.axis_index("gx") // NEAR * NEAR
    rows = sums_ref.shape[1] // 2
    fore = jnp.zeros((rows, LANES), F32)
    fores = []
    for k in range(NEAR):
        fores.append(fore)
        fore = sums_ref[k, :rows] + block_tab[0, start + k] * fore
    back = jnp.zeros((rows, LANES), F32)
    for k in reversed(range(NEAR)):
        back = (
            sums_ref[k, rows:]
            + block_tab[2, start + k] * fores[k]
            + block_tab[1, start + k] * back
        )
    for g in range(joined_out.shape[0]):
        joined_out[g, :rows] = fore
        joined_out[g, rows:] = back


def carry_kernel(block_tab, joined_ref, sums_ref, carry_out):
    own = lax.axis_index("gx") // NEAR
    start = own * NEAR
    groups = joined_ref.shape[0]
    rows = sums_ref.shape[1] // 2
    zero = jnp.zeros((rows, LANES), F32)
    fore, fore_own, fores, betas, gammas = zero, zero, [], [], []
    for g in range(groups):
        entries = [jnp.float32(1.0)]
        for k in range(NEAR):
            entries.append(entries[-1] * block_tab[0, g * NEAR + k])
        gamma, beta = jnp.float32(0.0), jnp.float32(1.0)
        for k in reversed(range(NEAR)):
            b = block_tab[1, g * NEAR + k]
            gamma = block_tab[2, g * NEAR + k] * entries[k] + b * gamma
            beta = beta * b
        gammas.append(gamma)
        betas.append(beta)
        fores.append(fore)
        fore_own = jnp.where(own == g, fore, fore_own)
        fore = joined_ref[g, :rows] + entries[NEAR] * fore
    back, back_own = zero, zero
    for g in reversed(range(groups)):
        back_own = jnp.where(own == g, back, back_own)
        back = joined_ref[g, rows:] + gammas[g] * fores[g] + betas[g] * back
    fore, back, fores = fore_own, back_own, []
    for k in range(NEAR):
        carry_out[k, :rows] = fore
        fores.append(fore)
        fore = sums_ref[k, :rows] + block_tab[0, start + k] * fore
    for k in reversed(range(NEAR)):
        carry_out[k, rows:] = back
        back = (
            sums_ref[k, rows:]
            + block_tab[2, start + k] * fores[k]
            + block_tab[1, start + k] * back
        )


def final_kernel(carry_ref, ends_ref, block_ref, out_ref):
    rows = carry_ref.shape[1] // 2
    fore = ends_ref[:CX]
    back = ends_ref[CX:]
    base = pl.program_id(0) * (rows * CX)
    for r in range(rows):
        out_ref[r * CX : (r + 1) * CX] = (
            block_ref[pl.ds(pl.multiple_of(base + r * CX, CX), CX), :]
            + carry_ref[0, r : r + 1] * fore
            + carry_ref[0, rows + r : rows + r + 1] * back
        )


def table(gap):
    decay = 1.0 - gap
    edge = jnp.zeros((1,), F32)
    prior = jnp.concatenate([edge, decay[:-1]])
    later = jnp.concatenate([decay[1:], edge])
    return jnp.stack([prior, later, jnp.sqrt(gap * (2.0 - gap))])


def call(kernel, outs, specs, scratch=()):
    shapes = tuple(jax.ShapeDtypeStruct(s, t) for s, t in outs)
    return pl.pallas_call(
        kernel,
        out_shape=shapes if len(shapes) > 1 else shapes[0],
        in_specs=specs,
        out_specs=(vmem,) * len(shapes) if len(shapes) > 1 else vmem,
        scratch_shapes=scratch,
        compiler_params=params(),
    )


def local(bin_resid, geometry, beam_weight, dest_device, dest_column, live_count, field_sigma, x_gap, y_gap):
    count_x = lax.axis_size("gx")
    count_y = lax.axis_size("gy")
    peers = count_x * count_y
    bins = bin_resid.shape[0]
    slots = SLOTS * peers
    far = count_x // NEAR
    chunk = 2 * DEPTH // NEAR
    near_groups = [[g * NEAR + k for k in range(NEAR)] for g in range(far)]
    far_groups = [[g * NEAR + k for g in range(far)] for k in range(NEAR)]
    side_groups = [[i * count_y + j for i in group for j in range(count_y)] for group in near_groups]
    a2a = functools.partial(lax.all_to_all, tiled=True)
    tie = lax.optimization_barrier

    def whole(*shape):
        return pl.BlockSpec(shape, lambda k: (0,) * len(shape))

    send = pl.pallas_call(
        pack_kernel,
        grid=(1,),
        out_shape=jax.ShapeDtypeStruct((peers, LANES), F32),
        in_specs=[
            smem,
            whole(1, bins),
            whole(1, bins),
            whole(1, bins),
            whole(FIELDS, bins),
            whole(LEVELS, bins),
        ],
        out_specs=whole(peers, LANES),
        compiler_params=params(),
    )(
        live_count,
        bin_resid.reshape(1, bins),
        dest_device.reshape(1, bins),
        dest_column.reshape(1, bins),
        geometry,
        beam_weight,
    )
    moved = a2a(send.reshape(far, peers // far, LANES), "gx", split_axis=0, concat_axis=0, axis_index_groups=far_groups)
    tab_x = table(x_gap)
    tab_y = table(y_gap)
    x_flat = tab_x.reshape(-1)
    sigma = jnp.broadcast_to(field_sigma.reshape(DEPTH, 1), (DEPTH, LANES))
    coefs = call(
        coef_kernel,
        [
            ((CY, CY), BF16),
            ((CY, CY), BF16),
            ((2, CY, LANES), F32),
            ((8, LANES), F32),
            ((8, LANES), F32),
            ((2 * CX, LANES), F32),
        ],
        [smem, smem, vmem, vmem, vmem],
        [pltpu.VMEM((CY, LANES), F32)] * 3,
    )(
        x_flat,
        tab_y.reshape(-1),
        tab_x.reshape(3, count_x, CX).transpose(0, 2, 1),
        tab_y.reshape(3, count_y, CY).transpose(0, 2, 1),
        tab_y.reshape(3, count_y, CY),
    )
    moved, coefs, sigma = tie((moved, coefs, sigma))
    dt_high, dt_low, tab, edge, blocks, x_ends = coefs
    moved = a2a(moved.transpose(1, 0, 2), ("gx", "gy"), split_axis=0, concat_axis=0, axis_index_groups=side_groups)
    moved = moved.reshape(peers, LANES)
    outer, column, ends = call(
        ends_kernel,
        [((2 * DEPTH, slots), BF16), ((1, slots), F32), ((count_y, DEPTH // 2, LANES), F32)],
        [vmem] * 3,
        [pltpu.VMEM((4 * DEPTH, slots), BF16)],
    )(moved, sigma, tab)
    ends = a2a(ends, "gy", split_axis=0, concat_axis=0)
    block, raw = call(
        grid_kernel,
        [((CX, DEPTH, LANES), F32), ((2, DEPTH, LANES), F32)],
        [smem] + [vmem] * 6,
        [pltpu.VMEM((8 * DEPTH, slots), BF16), pltpu.VMEM((slots, 2 * CY), BF16)],
    )(x_flat, outer, column, moved, sigma, dt_high, dt_low)
    both, sums = call(
        line_kernel,
        [((DEPTH, LANES), F32), ((NEAR, chunk, LANES), F32)],
        [smem, vmem, vmem, vmem],
    )(blocks, ends, edge, raw)
    sums = a2a(sums, "gx", split_axis=0, concat_axis=0, axis_index_groups=near_groups)
    joined = call(join_kernel, [((far, chunk, LANES), F32)], [smem, vmem])(blocks, sums)
    joined, block = tie((joined, block))
    joined = a2a(joined, "gx", split_axis=0, concat_axis=0, axis_index_groups=far_groups)
    block = call(
        scan_kernel,
        [((DEPTH * CX, LANES), F32)],
        [smem, vmem, vmem, vmem],
        [pltpu.VMEM((CX, DEPTH, LANES), F32)],
    )(x_flat, both, edge, block)
    carry = call(carry_kernel, [((NEAR, chunk, LANES), F32)], [smem, vmem, vmem])(blocks, joined, sums)
    carry = a2a(carry, "gx", split_axis=0, concat_axis=0, axis_index_groups=near_groups)
    rows = DEPTH * CX // NEAR
    out = pl.pallas_call(
        final_kernel,
        grid=(NEAR,),
        out_shape=jax.ShapeDtypeStruct((DEPTH * CX, LANES), F32),
        in_specs=[pl.BlockSpec((1, chunk, LANES), lambda k: (k, 0, 0)), vmem, vmem],
        out_specs=pl.BlockSpec((rows, LANES), lambda k: (k, 0)),
        compiler_params=params(),
    )(carry, x_ends, block)
    return out.reshape(FIELDS, LEVELS, CX, CY)


def solution(mesh):
    both = ("gx", "gy")
    placed = (P(both), P(None, both), P(None, both), P(both, None), P(both), P(both), P(), P(), P())
    return jax.shard_map(
        local, mesh=mesh, in_specs=placed, out_specs=P(None, None, "gx", "gy"), check_vma=False
    )
```

```python
import functools
import jax
import jax.numpy as jnp
from jax import lax
from jax.experimental import pallas as pl
from jax.experimental.pallas import tpu as pltpu
from jax.sharding import PartitionSpec as P

F32 = jnp.float32
BF16 = jnp.bfloat16
I32 = jnp.int32
LANES = 128
FIELDS = 6
LEVELS = 16
DEPTH = FIELDS * LEVELS
SLOTS = 4
WIDTH = 24
CX = 32
CY = 128
NEAR = 4
NX_GROUPS = 8
NY_BLOCKS = 16

params = functools.partial(pltpu.CompilerParams, vmem_limit_bytes=48 * 1024 * 1024)
vmem = pl.BlockSpec(memory_space=pltpu.VMEM)
smem = pl.BlockSpec(memory_space=pltpu.SMEM)
hbm = pl.BlockSpec(memory_space=pltpu.HBM)


def iota(shape, dim):
    return lax.broadcasted_iota(I32, shape, dim)


def split_two(values):
    high = values.astype(BF16)
    return high, (values - high.astype(F32)).astype(BF16)


def dot_nt(left, right):
    return lax.dot_general(left, right, (((1,), (1,)), ((), ())), preferred_element_type=F32)


def dot_nn(left, right):
    return lax.dot_general(left, right, (((1,), (0,)), ((), ())), preferred_element_type=F32)


def pack_kernel(live_ref, *refs):
    sources, (send_ref, *buffers, sems) = refs[:5], refs[5:]
    copies = [pltpu.make_async_copy(src, buf, sems.at[k]) for k, (src, buf) in enumerate(zip(sources, buffers))]
    for copy in copies:
        copy.start()
    for copy in copies:
        copy.wait()
    resid_ref, dest_ref, column_ref, geometry_ref, beam_ref = buffers
    bins = resid_ref.shape[1]
    peers = send_ref.shape[0]
    dest = dest_ref[...]
    dest_f = dest.astype(F32)
    dest_t = jnp.broadcast_to(dest_f, (LANES, bins)).T
    ranks = []
    for chunk in range(bins // LANES):
        rows = (chunk + 1) * LANES
        same = dest_t[:rows] == dest_f[:, chunk * LANES : rows]
        before = iota((rows, LANES), 0) < iota((rows, LANES), 1) + chunk * LANES
        ranks.append(jnp.sum(jnp.where(same & before, 1.0, 0.0), axis=0, keepdims=True))
    rank = jnp.concatenate(ranks, axis=1)
    alive = jnp.where(iota((1, bins), 1) < live_ref[0], 1.0, 0.0)
    weighted = geometry_ref[...] * (alive * resid_ref[...])
    payload = jnp.concatenate(
        [
            beam_ref[...],
            weighted,
            column_ref[...].astype(F32),
            jnp.zeros((WIDTH - LEVELS - FIELDS - 1, bins), F32),
        ],
        axis=0,
    )
    spread = jnp.concatenate([jnp.where(rank == float(s), payload, 0.0) for s in range(SLOTS)], axis=0)
    high = spread.astype(BF16)
    rest = spread - high.astype(F32)
    middle = rest.astype(BF16)
    low = (rest - middle.astype(F32)).astype(BF16)
    onehot = jnp.where(iota((peers, bins), 0) == dest, 1.0, 0.0).astype(BF16)
    send_ref[...] = dot_nt(onehot, high) + (dot_nt(onehot, middle) + dot_nt(onehot, low))


def coef_kernel(x_flat, y_flat, x_cols, y_cols, y_rows, dt_high, dt_low, tab_ref, edge_ref, block_ref, ends_ref, chain, gammas, betas):
    own_x = lax.axis_index("gx")
    own_y = lax.axis_index("gy")
    length = y_rows.shape[1] * LANES
    span = x_cols.shape[2] * CX

    def block_scalars(cols, row):
        steps, blocks = cols.shape[1:]

        def forward(p, value):
            value = value * cols[0, pl.ds(p, 1), :]
            gammas[pl.ds(p, 1), :blocks] = value
            return value

        alpha = lax.fori_loop(0, steps, forward, jnp.ones((1, blocks), F32))

        def backward(k, carried):
            gamma, beta = carried
            p = steps - 1 - k
            later = cols[1, pl.ds(p, 1), :]
            gamma = cols[2, pl.ds(p, 1), :] * gammas[pl.ds(p, 1), :blocks] + later * gamma
            beta = beta * later
            gammas[pl.ds(p, 1), :blocks] = gamma
            betas[pl.ds(p, 1), :blocks] = beta
            return gamma, beta

        gamma, beta = lax.fori_loop(
            0, steps, backward, (jnp.zeros((1, blocks), F32), jnp.ones((1, blocks), F32))
        )
        block_ref[row : row + 1, :blocks] = alpha
        block_ref[row + 1 : row + 2, :blocks] = beta
        block_ref[row + 2 : row + 3, :blocks] = gamma

    block_ref[...] = jnp.zeros(block_ref.shape, F32)
    block_scalars(y_cols, 3)
    block_scalars(x_cols, 0)
    blocks = x_cols.shape[2]
    mine = iota((CX, blocks), 1) == own_x
    for k, scratch in enumerate((gammas, betas)):
        picked = jnp.where(mine, scratch[:CX, :blocks] * x_cols[2], 0.0)
        ends_ref[k * CX : (k + 1) * CX] = jnp.broadcast_to(
            jnp.sum(picked, axis=1, keepdims=True), (CX, LANES)
        )

    lane = iota((1, LANES), 1)
    first = own_x * CX
    down = []
    weight = jnp.float32(1.0)
    for x in range(CX):
        down.append(weight * x_flat[2 * span + first + x])
        weight = weight * x_flat[span + first + x]
    tail, start = jnp.float32(1.0), down[CX - 1]
    tails, starts = [tail], [start]
    for x in reversed(range(CX - 1)):
        factor = x_flat[first + x + 1]
        tail = tail * factor
        start = down[x] + factor * start
        tails.append(tail)
        starts.append(start)
    row_tail = jnp.zeros((1, LANES), F32)
    row_start = jnp.zeros((1, LANES), F32)
    for x in range(CX):
        row_tail = jnp.where(lane % CX == x, tails[CX - 1 - x], row_tail)
        row_start = jnp.where(lane % CX == x, starts[CX - 1 - x], row_start)

    first = own_y * CY

    def fill(n, row):
        row = jnp.where(lane == n, 1.0, row * y_flat[first + n])
        chain[pl.ds(n, 1), :] = row
        return row

    lax.fori_loop(0, CY, fill, jnp.zeros((1, LANES), F32))

    def unfill(k, row):
        n = CY - 1 - k
        row = chain[pl.ds(n, 1), :] * y_flat[2 * length + first + n] + row * y_flat[length + first + n]
        chain[pl.ds(n, 1), :] = row
        return row

    lax.fori_loop(0, CY, unfill, jnp.zeros((1, LANES), F32))
    scale = y_rows[2, pl.ds(own_y, 1), :]
    filt = chain[...].T * scale
    high, low = split_two(filt)
    dt_high[...] = high
    dt_low[...] = low
    scale_first = scale[:, :1]
    scale_last = scale[:, CY - 1 :]
    tab_ref[0] = jnp.broadcast_to(filt[:, CY - 1 :] / (scale_last * scale_last), (CY, LANES))
    tab_ref[1] = jnp.broadcast_to(filt[:, :1] / scale_first, (CY, LANES))
    edge_ref[...] = jnp.zeros(edge_ref.shape, F32)
    edge_ref[0:1] = filt[:1] * y_flat[first]
    edge_ref[1:2] = filt[CY - 1 :] * y_flat[length + first + CY - 1] / scale_last
    edge_ref[2:3] = row_tail
    edge_ref[3:4] = row_start


def ends_kernel(scalars, recv_ref, sigma_ref, tab_ref, outer_out, column_out, ends_out, outer):
    sources = recv_ref.shape[0]
    turned = recv_ref[...].T
    weights = [jnp.concatenate([tab_ref[c]] * (sources // LANES), axis=1) for c in range(2)]
    hits = []
    for s in range(SLOTS):
        at = slice(s * sources, (s + 1) * sources)
        base = s * WIDTH
        beam = turned[base : base + LEVELS]
        place = turned[base + LEVELS + FIELDS : base + LEVELS + FIELDS + 1]
        column_out[:, at] = place
        place = place.astype(I32)
        on_y = iota((CY, sources), 0) == (place & (CY - 1))
        ends = [jnp.sum(jnp.where(on_y, w, 0.0), axis=0, keepdims=True) for w in weights]
        hits.append(jnp.where((iota((LANES, sources), 0) & (CX - 1)) == (place >> 7), 1.0, 0.0).astype(BF16))
        for f in range(FIELDS):
            prod = beam * turned[base + LEVELS + f : base + LEVELS + f + 1]
            rows = slice(f * LEVELS, (f + 1) * LEVELS)
            high, low = split_two(prod)
            outer_out[rows, at] = high
            outer_out[DEPTH + f * LEVELS : DEPTH + (f + 1) * LEVELS, at] = low
            for c in range(2):
                high, low = split_two(prod * ends[c])
                outer[(2 * c) * DEPTH + f * LEVELS : (2 * c) * DEPTH + (f + 1) * LEVELS, at] = high
                outer[(2 * c + 1) * DEPTH + f * LEVELS : (2 * c + 1) * DEPTH + (f + 1) * LEVELS, at] = low
    summed = dot_nt(outer[...], jnp.concatenate(hits, axis=1))
    sigma = sigma_ref[...]
    fore = (summed[:DEPTH] + summed[DEPTH : 2 * DEPTH]) * sigma
    back = (summed[2 * DEPTH : 3 * DEPTH] + summed[3 * DEPTH :]) * sigma
    own = lax.axis_index("gy")
    back = back + scalars[4, own] * fore
    rows = DEPTH // 4
    quarter = iota((rows, LANES), 1) // CX
    fore_row, back_row = fore[:rows], back[:rows]
    for q in range(1, 4):
        at = slice(q * rows, (q + 1) * rows)
        fore_row = jnp.where(quarter == q, fore[at], fore_row)
        back_row = jnp.where(quarter == q, back[at], back_row)
    for j in range(ends_out.shape[0]):
        ends_out[j] = jnp.where(own <= j, fore_row, back_row)


def grid_kernel(x_flat, outer_ref, column_ref, recv_ref, sigma_ref, dt_high, dt_low, block_out, sums_out, masked, hit):
    sources = recv_ref.shape[0]
    first = lax.axis_index("gx") * CX
    length = x_flat.shape[0] // 3
    lane2 = iota((1, 2 * LANES), 1)
    for s in range(SLOTS):
        place = s * WIDTH + LEVELS + FIELDS
        cols = jnp.broadcast_to(recv_ref[:, place : place + 1], (sources, LANES)).astype(I32) & (2 * CY - 1)
        cols = jnp.concatenate([cols, cols], axis=1)
        hit[s * sources : (s + 1) * sources] = jnp.where(cols == lane2, 1.0, 0.0).astype(BF16)
    pair = column_ref[...].astype(I32) >> 8
    sigma = sigma_ref[...]
    group = 4

    def step(n, carried):
        run, begin, weight = carried
        for c in range(group):
            keep = jnp.where(pair == n * group + c, 1.0, 0.0)
            keep = jnp.broadcast_to(keep, (16, keep.shape[1])).astype(BF16)
            for r in range(2 * DEPTH // 16):
                masked[c * 2 * DEPTH + r * 16 : c * 2 * DEPTH + (r + 1) * 16] = (
                    outer_ref[r * 16 : (r + 1) * 16] * keep
                )
        summed = dot_nn(masked[...], hit[...])
        parts = []
        for c in range(group):
            both = summed[c * 2 * DEPTH : c * 2 * DEPTH + DEPTH] + summed[c * 2 * DEPTH + DEPTH : (c + 1) * 2 * DEPTH]
            parts += [both[:, :CY] * sigma, both[:, CY:] * sigma]
        high, low = split_two(jnp.concatenate(parts, axis=0))
        passed = dot_nn(high, dt_high[...]) + (dot_nn(low, dt_high[...]) + dot_nn(high, dt_low[...]))
        for h in range(2 * group):
            part = passed[h * DEPTH : (h + 1) * DEPTH]
            x = n * 2 * group + h
            block_out[x] = part
            run = part + jnp.where(x == 0, 0.0, x_flat[first + x]) * run
            begin = begin + (weight * x_flat[2 * length + first + x]) * run
            weight = weight * x_flat[length + first + x]
        return run, begin, weight

    zero = jnp.zeros((DEPTH, LANES), F32)
    run, begin, _ = lax.fori_loop(0, CX // (2 * group), step, (zero, zero, jnp.float32(1.0)))
    sums_out[0] = run
    sums_out[1] = begin


def line_kernel(block_tab, scalars, ends_ref, edge_ref, raw_ref, both_out, sums_out):
    own = lax.axis_index("gy")
    count, rows, _ = ends_ref.shape
    fore = jnp.zeros((rows, LANES), F32)
    for j in range(count - 1):
        fore = jnp.where(j < own, ends_ref[j] + block_tab[3, j] * fore, fore)
    back = jnp.zeros((rows, LANES), F32)
    for j in reversed(range(1, count)):
        back = jnp.where(j > own, ends_ref[j] + block_tab[4, j] * back, back)
    back = back + scalars[3, own + 1] * (ends_ref[own] + block_tab[3, own] * fore)
    lane = iota((DEPTH, LANES), 1)
    parts = []
    for q in range(4):
        left = fore if q == 0 else pltpu.roll(fore, LANES - q * CX, 1)
        right = back if q == 1 else pltpu.roll(back, (LANES - q * CX + CX) % LANES, 1)
        parts.append(jnp.where(lane[:rows] < CX, left, right))
    both = jnp.concatenate(parts, axis=0)
    both_out[...] = both
    edge_fore = edge_ref[0:1]
    edge_back = edge_ref[1:2]
    rows = DEPTH // NEAR
    for c in range(2):
        weighted = both * edge_ref[2 + c : 3 + c]
        fore_part = jnp.sum(jnp.where(lane < CX, weighted, 0.0), axis=1, keepdims=True)
        back_part = jnp.sum(jnp.where((lane >= CX) & (lane < 2 * CX), weighted, 0.0), axis=1, keepdims=True)
        total = raw_ref[c] + fore_part * edge_fore + back_part * edge_back
        for k in range(NEAR):
            sums_out[k, c * rows : (c + 1) * rows] = total[k * rows : (k + 1) * rows]


def scan_kernel(x_flat, both_ref, edge_ref, block_ref, out_ref, scaled):
    first = lax.axis_index("gx") * CX
    length = x_flat.shape[0] // 3
    both = both_ref[...]
    edge_fore = edge_ref[0:1]
    edge_back = edge_ref[1:2]
    run = jnp.zeros((DEPTH, LANES), F32)
    for x in range(CX):
        part = block_ref[x] + both[:, x : x + 1] * edge_fore + both[:, CX + x : CX + x + 1] * edge_back
        run = part if x == 0 else part + x_flat[first + x] * run
        scaled[x] = x_flat[2 * length + first + x] * run
    back = jnp.zeros((DEPTH, LANES), F32)
    for x in reversed(range(CX)):
        back = scaled[x] if x == CX - 1 else scaled[x] + x_flat[length + first + x] * back
        out_ref[pl.ds(x, DEPTH, stride=CX), :] = x_flat[2 * length + first + x] * back


def chain_kernel(block_tab, out):
    groups = NX_GROUPS
    zero, one = jnp.float32(0.0), jnp.float32(1.0)
    out[2, groups] = zero
    for g in reversed(range(groups)):
        entries = [one]
        for k in range(NEAR):
            entries.append(entries[-1] * block_tab[0, g * NEAR + k])
        gamma, beta = zero, one
        for k in reversed(range(NEAR)):
            step = block_tab[1, g * NEAR + k]
            gamma = block_tab[2, g * NEAR + k] * entries[k] + step * gamma
            beta = beta * step
        out[0, g] = entries[NEAR]
        out[1, g] = beta
        out[5, g] = beta * out[2, g + 1]
        out[2, g] = gamma + beta * entries[NEAR] * out[2, g + 1]
    blocks = NY_BLOCKS
    out[3, blocks] = zero
    for j in reversed(range(blocks)):
        beta = block_tab[4, j]
        out[4, j] = beta * out[3, j + 1]
        out[3, j] = block_tab[5, j] + beta * block_tab[3, j] * out[3, j + 1]


def join_kernel(block_tab, scalars, sums_ref, joined_out):
    own = lax.axis_index("gx") // NEAR
    start = own * NEAR
    rows = sums_ref.shape[1] // 2
    fore = jnp.zeros((rows, LANES), F32)
    fores = []
    for k in range(NEAR):
        fores.append(fore)
        fore = sums_ref[k, :rows] + block_tab[0, start + k] * fore
    back = jnp.zeros((rows, LANES), F32)
    for k in reversed(range(NEAR)):
        back = (
            sums_ref[k, rows:]
            + block_tab[2, start + k] * fores[k]
            + block_tab[1, start + k] * back
        )
    back = back + scalars[5, own] * fore
    for g in range(joined_out.shape[0]):
        joined_out[g] = jnp.where(own <= g, fore, back)


def carry_kernel(block_tab, scalars, joined_ref, sums_ref, carry_out):
    own = lax.axis_index("gx") // NEAR
    start = own * NEAR
    groups, rows, _ = joined_ref.shape
    fore = jnp.zeros((rows, LANES), F32)
    for g in range(groups - 1):
        fore = jnp.where(g < own, joined_ref[g] + scalars[0, g] * fore, fore)
    back = jnp.zeros((rows, LANES), F32)
    for g in reversed(range(1, groups)):
        back = jnp.where(g > own, joined_ref[g] + scalars[1, g] * back, back)
    back = back + scalars[2, own + 1] * (joined_ref[own] + scalars[0, own] * fore)
    fores = []
    for k in range(NEAR):
        carry_out[k, :rows] = fore
        fores.append(fore)
        fore = sums_ref[k, :rows] + block_tab[0, start + k] * fore
    for k in reversed(range(NEAR)):
        carry_out[k, rows:] = back
        back = (
            sums_ref[k, rows:]
            + block_tab[2, start + k] * fores[k]
            + block_tab[1, start + k] * back
        )


def final_kernel(carry_ref, ends_ref, block_ref, out_ref):
    rows = carry_ref.shape[1] // 2
    fore = ends_ref[:CX]
    back = ends_ref[CX:]
    base = pl.program_id(0) * (rows * CX)
    for r in range(rows):
        out_ref[r * CX : (r + 1) * CX] = (
            block_ref[pl.ds(pl.multiple_of(base + r * CX, CX), CX), :]
            + carry_ref[0, r : r + 1] * fore
            + carry_ref[0, rows + r : rows + r + 1] * back
        )


def table(gap):
    decay = 1.0 - gap
    edge = jnp.zeros((1,), F32)
    prior = jnp.concatenate([edge, decay[:-1]])
    later = jnp.concatenate([decay[1:], edge])
    return jnp.stack([prior, later, jnp.sqrt(gap * (2.0 - gap))])


def call(kernel, outs, specs, scratch=()):
    shapes = tuple(jax.ShapeDtypeStruct(s, t) for s, t in outs)
    return pl.pallas_call(
        kernel,
        out_shape=shapes if len(shapes) > 1 else shapes[0],
        in_specs=specs,
        out_specs=(vmem,) * len(shapes) if len(shapes) > 1 else vmem,
        scratch_shapes=scratch,
        compiler_params=params(),
    )


def local(bin_resid, geometry, beam_weight, dest_device, dest_column, live_count, field_sigma, x_gap, y_gap):
    count_x = lax.axis_size("gx")
    count_y = lax.axis_size("gy")
    peers = count_x * count_y
    bins = bin_resid.shape[0]
    slots = SLOTS * peers
    far = count_x // NEAR
    chunk = 2 * DEPTH // NEAR
    near_groups = [[g * NEAR + k for k in range(NEAR)] for g in range(far)]
    far_groups = [[g * NEAR + k for g in range(far)] for k in range(NEAR)]
    side_groups = [[i * count_y + j for i in group for j in range(count_y)] for group in near_groups]
    a2a = functools.partial(lax.all_to_all, tiled=True)
    tie = lax.optimization_barrier

    row = (1, bins)
    send = call(
        pack_kernel,
        [((peers, SLOTS * WIDTH), F32)],
        [smem] + [hbm] * 5,
        [
            pltpu.VMEM(row, F32),
            pltpu.VMEM(row, I32),
            pltpu.VMEM(row, I32),
            pltpu.VMEM((FIELDS, bins), F32),
            pltpu.VMEM((LEVELS, bins), F32),
            pltpu.SemaphoreType.DMA((5,)),
        ],
    )(
        live_count,
        bin_resid.reshape(row),
        dest_device.reshape(row),
        dest_column.reshape(row),
        geometry,
        beam_weight,
    )
    moved = a2a(send.reshape(far, peers // far, SLOTS * WIDTH), "gx", split_axis=0, concat_axis=0, axis_index_groups=far_groups)
    tab_x = table(x_gap)
    tab_y = table(y_gap)
    x_flat = tab_x.reshape(-1)
    sigma = jnp.broadcast_to(field_sigma.reshape(DEPTH, 1), (DEPTH, LANES))
    coefs = call(
        coef_kernel,
        [
            ((CY, CY), BF16),
            ((CY, CY), BF16),
            ((2, CY, LANES), F32),
            ((8, LANES), F32),
            ((8, LANES), F32),
            ((2 * CX, LANES), F32),
        ],
        [smem, smem, vmem, vmem, vmem],
        [pltpu.VMEM((CY, LANES), F32)] * 3,
    )(
        x_flat,
        tab_y.reshape(-1),
        tab_x.reshape(3, count_x, CX).transpose(0, 2, 1),
        tab_y.reshape(3, count_y, CY).transpose(0, 2, 1),
        tab_y.reshape(3, count_y, CY),
    )
    scalars = pl.pallas_call(
        chain_kernel,
        out_shape=jax.ShapeDtypeStruct((6, LANES), F32),
        in_specs=[smem],
        out_specs=smem,
        compiler_params=params(),
    )(coefs[4])
    moved, coefs, sigma, scalars = tie((moved, coefs, sigma, scalars))
    dt_high, dt_low, tab, edge, blocks, x_ends = coefs
    moved = a2a(moved.transpose(1, 0, 2), ("gx", "gy"), split_axis=0, concat_axis=0, axis_index_groups=side_groups)
    moved = moved.reshape(peers, SLOTS * WIDTH)
    outer, column, ends = call(
        ends_kernel,
        [((2 * DEPTH, slots), BF16), ((1, slots), F32), ((count_y, DEPTH // 4, LANES), F32)],
        [smem] + [vmem] * 3,
        [pltpu.VMEM((4 * DEPTH, slots), BF16)],
    )(scalars, moved, sigma, tab)
    ends = a2a(ends, "gy", split_axis=0, concat_axis=0)
    block, raw = call(
        grid_kernel,
        [((CX, DEPTH, LANES), F32), ((2, DEPTH, LANES), F32)],
        [smem] + [vmem] * 6,
        [pltpu.VMEM((8 * DEPTH, slots), BF16), pltpu.VMEM((slots, 2 * CY), BF16)],
    )(x_flat, outer, column, moved, sigma, dt_high, dt_low)
    both, sums = call(
        line_kernel,
        [((DEPTH, LANES), F32), ((NEAR, chunk, LANES), F32)],
        [smem, smem, vmem, vmem, vmem],
    )(blocks, scalars, ends, edge, raw)
    sums = a2a(sums, "gx", split_axis=0, concat_axis=0, axis_index_groups=near_groups)
    joined = call(join_kernel, [((far, chunk // 2, LANES), F32)], [smem, smem, vmem])(blocks, scalars, sums)
    joined, block = tie((joined, block))
    joined = a2a(joined, "gx", split_axis=0, concat_axis=0, axis_index_groups=far_groups)
    block = call(
        scan_kernel,
        [((DEPTH * CX, LANES), F32)],
        [smem, vmem, vmem, vmem],
        [pltpu.VMEM((CX, DEPTH, LANES), F32)],
    )(x_flat, both, edge, block)
    joined, block = tie((joined, block))
    carry = call(carry_kernel, [((NEAR, chunk, LANES), F32)], [smem, smem, vmem, vmem])(
        blocks, scalars, joined, sums
    )
    carry = a2a(carry, "gx", split_axis=0, concat_axis=0, axis_index_groups=near_groups)
    rows = DEPTH * CX // NEAR
    out = pl.pallas_call(
        final_kernel,
        grid=(NEAR,),
        out_shape=jax.ShapeDtypeStruct((DEPTH * CX, LANES), F32),
        in_specs=[pl.BlockSpec((1, chunk, LANES), lambda k: (k, 0, 0)), vmem, vmem],
        out_specs=pl.BlockSpec((rows, LANES), lambda k: (k, 0)),
        compiler_params=params(),
    )(carry, x_ends, block)
    return out.reshape(FIELDS, LEVELS, CX, CY)


def solution(mesh):
    both = ("gx", "gy")
    placed = (P(both), P(None, both), P(None, both), P(both, None), P(both), P(both), P(), P(), P())
    return jax.shard_map(
        local, mesh=mesh, in_specs=placed, out_specs=P(None, None, "gx", "gy"), check_vma=False
    )
```

```python
import functools
import jax
import jax.numpy as jnp
from jax import lax
from jax.experimental import pallas as pl
from jax.experimental.pallas import tpu as pltpu
from jax.sharding import PartitionSpec as P

F32 = jnp.float32
BF16 = jnp.bfloat16
I32 = jnp.int32
LANES = 128
FIELDS = 6
LEVELS = 16
DEPTH = FIELDS * LEVELS
SLOTS = 4
WIDTH = 24
CX = 32
CY = 128
NEAR = 4
NX_GROUPS = 8
NX_BLOCKS = NX_GROUPS * NEAR
NY_BLOCKS = 16
ALPHA_X, BETA_X, GAMMA_X = 0, 32, 64
ALPHA_Y, BETA_Y, FOLD_Y, TURN_Y = 96, 112, 128, 152
ALPHA_G, BETA_G, FOLD_G, TURN_G = 168, 176, 184, 200
TAB_ROWS = 208


def params(mib=48):
    return pltpu.CompilerParams(vmem_limit_bytes=mib * 1024 * 1024)


vmem = pl.BlockSpec(memory_space=pltpu.VMEM)
smem = pl.BlockSpec(memory_space=pltpu.SMEM)
hbm = pl.BlockSpec(memory_space=pltpu.HBM)


def iota(shape, dim):
    return lax.broadcasted_iota(I32, shape, dim)


def split_two(values):
    high = values.astype(BF16)
    return high, (values - high.astype(F32)).astype(BF16)


def dot_nt(left, right):
    return lax.dot_general(left, right, (((1,), (1,)), ((), ())), preferred_element_type=F32)


def dot_nn(left, right):
    return lax.dot_general(left, right, (((1,), (0,)), ((), ())), preferred_element_type=F32)


def pack_kernel(live_ref, *refs):
    sources, (send_ref, *buffers, sems) = refs[:5], refs[5:]
    copies = [pltpu.make_async_copy(src, buf, sems.at[k]) for k, (src, buf) in enumerate(zip(sources, buffers))]
    for copy in copies:
        copy.start()
    for copy in copies:
        copy.wait()
    resid_ref, dest_ref, column_ref, geometry_ref, beam_ref = buffers
    bins = resid_ref.shape[1]
    peers = send_ref.shape[0]
    dest = dest_ref[...]
    dest_f = dest.astype(F32)
    dest_t = jnp.broadcast_to(dest_f, (LANES, bins)).T
    ranks = []
    for chunk in range(bins // LANES):
        rows = (chunk + 1) * LANES
        same = dest_t[:rows] == dest_f[:, chunk * LANES : rows]
        before = iota((rows, LANES), 0) < iota((rows, LANES), 1) + chunk * LANES
        ranks.append(jnp.sum(jnp.where(same & before, 1.0, 0.0), axis=0, keepdims=True))
    rank = jnp.concatenate(ranks, axis=1)
    alive = jnp.where(iota((1, bins), 1) < live_ref[0], 1.0, 0.0)
    weighted = geometry_ref[...] * (alive * resid_ref[...])
    payload = jnp.concatenate(
        [
            beam_ref[...],
            weighted,
            column_ref[...].astype(F32),
            jnp.zeros((WIDTH - LEVELS - FIELDS - 1, bins), F32),
        ],
        axis=0,
    )
    spread = jnp.concatenate([jnp.where(rank == float(s), payload, 0.0) for s in range(SLOTS)], axis=0)
    high = spread.astype(BF16)
    rest = spread - high.astype(F32)
    middle = rest.astype(BF16)
    low = (rest - middle.astype(F32)).astype(BF16)
    onehot = jnp.where(iota((peers, bins), 0) == dest, 1.0, 0.0).astype(BF16)
    send_ref[...] = dot_nt(onehot, high) + (dot_nt(onehot, middle) + dot_nt(onehot, low))


def coef_kernel(x_flat, y_flat, x_cols, y_cols, y_rows, mat_ref, tab_ref, edge_ref, block_ref, ends_ref, chain, gammas, betas):
    own_x = lax.axis_index("gx")
    own_y = lax.axis_index("gy")
    length = y_rows.shape[1] * LANES
    span = x_cols.shape[2] * CX

    def block_scalars(cols, row):
        steps, blocks = cols.shape[1:]

        def forward(p, value):
            value = value * cols[0, pl.ds(p, 1), :]
            gammas[pl.ds(p, 1), :blocks] = value
            return value

        alpha = lax.fori_loop(0, steps, forward, jnp.ones((1, blocks), F32))

        def backward(k, carried):
            gamma, beta = carried
            p = steps - 1 - k
            later = cols[1, pl.ds(p, 1), :]
            gamma = cols[2, pl.ds(p, 1), :] * gammas[pl.ds(p, 1), :blocks] + later * gamma
            beta = beta * later
            gammas[pl.ds(p, 1), :blocks] = gamma
            betas[pl.ds(p, 1), :blocks] = beta
            return gamma, beta

        gamma, beta = lax.fori_loop(
            0, steps, backward, (jnp.zeros((1, blocks), F32), jnp.ones((1, blocks), F32))
        )
        block_ref[row : row + 1, :blocks] = alpha
        block_ref[row + 1 : row + 2, :blocks] = beta
        block_ref[row + 2 : row + 3, :blocks] = gamma

    block_ref[...] = jnp.zeros(block_ref.shape, F32)
    block_scalars(y_cols, 3)
    block_scalars(x_cols, 0)
    blocks = x_cols.shape[2]
    mine = iota((CX, blocks), 1) == own_x
    for k, scratch in enumerate((gammas, betas)):
        picked = jnp.where(mine, scratch[:CX, :blocks] * x_cols[2], 0.0)
        ends_ref[k * CX : (k + 1) * CX] = jnp.broadcast_to(
            jnp.sum(picked, axis=1, keepdims=True), (CX, LANES)
        )

    lane = iota((1, LANES), 1)
    first = own_x * CX
    down = []
    weight = jnp.float32(1.0)
    for x in range(CX):
        down.append(weight * x_flat[2 * span + first + x])
        weight = weight * x_flat[span + first + x]
    tail, start = jnp.float32(1.0), down[CX - 1]
    tails, starts = [tail], [start]
    for x in reversed(range(CX - 1)):
        factor = x_flat[first + x + 1]
        tail = tail * factor
        start = down[x] + factor * start
        tails.append(tail)
        starts.append(start)
    row_tail = jnp.zeros((1, LANES), F32)
    row_start = jnp.zeros((1, LANES), F32)
    for x in range(CX):
        row_tail = jnp.where(lane % CX == x, tails[CX - 1 - x], row_tail)
        row_start = jnp.where(lane % CX == x, starts[CX - 1 - x], row_start)

    first = own_y * CY

    def fill(n, row):
        row = jnp.where(lane == n, 1.0, row * y_flat[first + n])
        chain[pl.ds(n, 1), :] = row
        return row

    lax.fori_loop(0, CY, fill, jnp.zeros((1, LANES), F32))

    def unfill(k, row):
        n = CY - 1 - k
        row = chain[pl.ds(n, 1), :] * y_flat[2 * length + first + n] + row * y_flat[length + first + n]
        chain[pl.ds(n, 1), :] = row
        return row

    lax.fori_loop(0, CY, unfill, jnp.zeros((1, LANES), F32))
    scale = y_rows[2, pl.ds(own_y, 1), :]
    filt = chain[...].T * scale
    high, low = split_two(filt)
    mat_ref[:CY, :CY] = high
    mat_ref[:CY, CY:] = low
    mat_ref[CY:, :CY] = high
    mat_ref[CY:, CY:] = jnp.zeros((CY, CY), BF16)
    scale_first = scale[:, :1]
    scale_last = scale[:, CY - 1 :]
    tab_ref[0] = jnp.broadcast_to(filt[:, CY - 1 :] / (scale_last * scale_last), (CY, LANES))
    tab_ref[1] = jnp.broadcast_to(filt[:, :1] / scale_first, (CY, LANES))
    edge_ref[...] = jnp.zeros(edge_ref.shape, F32)
    edge_ref[0:1] = filt[:1] * y_flat[first]
    edge_ref[1:2] = filt[CY - 1 :] * y_flat[length + first + CY - 1] / scale_last
    edge_ref[2:3] = row_tail
    edge_ref[3:4] = row_start
    for c, row in enumerate((row_tail, row_start)):
        tab_ref[2 + c] = jnp.broadcast_to(jnp.where(lane < CX, row, 0.0), (LANES, LANES)).T


def weigh(turned, weights, outer):
    sources = turned.shape[1]
    for s in range(SLOTS):
        at = slice(s * sources, (s + 1) * sources)
        base = s * WIDTH
        for f in range(FIELDS):
            prod = turned[base : base + LEVELS] * turned[base + LEVELS + f : base + LEVELS + f + 1]
            for c in range(2):
                high, low = split_two(prod * weights[s][c])
                row = 2 * c * DEPTH + f * LEVELS
                outer[row : row + LEVELS, at] = high
                outer[row + DEPTH : row + DEPTH + LEVELS, at] = low


def weighted_sums(outer, hits, sigma):
    summed = dot_nt(outer[...], jnp.concatenate(hits, axis=1))
    return [(summed[k : k + DEPTH] + summed[k + DEPTH : k + 2 * DEPTH]) * sigma for k in (0, 2 * DEPTH)]


def on_lines(turned, s):
    row = s * WIDTH + LEVELS + FIELDS
    place = turned[row : row + 1].astype(I32)
    on_y = iota((CY, place.shape[1]), 0) == (place & (CY - 1))
    on_x = (iota((LANES, place.shape[1]), 0) & (CX - 1)) == (place >> 7)
    return on_x, on_y


def pick(on_line, column):
    return jnp.sum(jnp.where(on_line, column, 0.0), axis=0, keepdims=True)


def as_bits(on_line):
    return jnp.where(on_line, 1.0, 0.0).astype(BF16)


def ends_kernel(recv_ref, sigma_ref, tab_ref, scalars, turned_out, ends_out, outer):
    sources = recv_ref.shape[0]
    turned = recv_ref[...].T
    turned_out[...] = turned
    columns = [jnp.concatenate([tab_ref[c]] * (sources // LANES), axis=1) for c in range(2)]
    hits, weights = [], []
    for s in range(SLOTS):
        on_x, on_y = on_lines(turned, s)
        hits.append(as_bits(on_x))
        weights.append([pick(on_y, column) for column in columns])
    weigh(turned, weights, outer)
    fore, back = weighted_sums(outer, hits, sigma_ref[...])
    own = lax.axis_index("gy")
    back = back + scalars[pl.ds(TURN_Y + own, 1), :] * fore
    rows = DEPTH // 4
    quarter = iota((rows, LANES), 1) // CX
    fore_row, back_row = fore[:rows], back[:rows]
    for q in range(1, 4):
        at = slice(q * rows, (q + 1) * rows)
        fore_row = jnp.where(quarter == q, fore[at], fore_row)
        back_row = jnp.where(quarter == q, back[at], back_row)
    for j in range(ends_out.shape[0]):
        ends_out[j] = jnp.where(own <= j, fore_row, back_row)


def sums_kernel(turned_ref, sigma_ref, tab_ref, mat_ref, sums_out, outer):
    turned = turned_ref[...]
    sources = turned.shape[1]
    columns = [jnp.concatenate([tab_ref[2 + c]] * (sources // LANES), axis=1) for c in range(2)]
    hits, weights = [], []
    for s in range(SLOTS):
        on_x, on_y = on_lines(turned, s)
        hits.append(as_bits(on_y))
        weights.append([pick(on_x, column) for column in columns])
    weigh(turned, weights, outer)
    both = jnp.concatenate(weighted_sums(outer, hits, sigma_ref[...]), axis=0)
    both = y_filter(both, mat_ref)
    sums_out[0] = both[:DEPTH]
    sums_out[1] = both[DEPTH:]


def y_filter(values, mat_ref):
    passed = dot_nn(jnp.concatenate(split_two(values), axis=1), mat_ref[...])
    return passed[:, :CY] + passed[:, CY:]


def grid_kernel(x_flat, turned_ref, recv_ref, sigma_ref, mat_ref, both_ref, edge_ref, out_ref, outer, masked, hit, scaled):
    sources = recv_ref.shape[0]
    first = lax.axis_index("gx") * CX
    length = x_flat.shape[0] // 3
    lane2 = iota((1, 2 * LANES), 1)
    pairs = []
    for s in range(SLOTS):
        at = slice(s * sources, (s + 1) * sources)
        base = s * WIDTH
        place = base + LEVELS + FIELDS
        cols = jnp.broadcast_to(recv_ref[:, place : place + 1], (sources, LANES)).astype(I32) & (2 * CY - 1)
        cols = jnp.concatenate([cols, cols], axis=1)
        hit[at] = as_bits(cols == lane2)
        pairs.append(turned_ref[place : place + 1].astype(I32) >> 8)
        for f in range(FIELDS):
            high, low = split_two(
                turned_ref[base : base + LEVELS] * turned_ref[base + LEVELS + f : base + LEVELS + f + 1]
            )
            outer[f * LEVELS : (f + 1) * LEVELS, at] = high
            outer[DEPTH + f * LEVELS : DEPTH + (f + 1) * LEVELS, at] = low
    pair = jnp.concatenate(pairs, axis=1)
    sigma = sigma_ref[...]
    both = both_ref[...]
    edge_fore = edge_ref[0:1]
    edge_back = edge_ref[1:2]
    lane = iota((DEPTH, LANES), 1)
    group = 4

    def step(n, run):
        for c in range(group):
            keep = jnp.where(pair == n * group + c, 1.0, 0.0)
            keep = jnp.broadcast_to(keep, (16, keep.shape[1])).astype(BF16)
            for r in range(2 * DEPTH // 16):
                masked[c * 2 * DEPTH + r * 16 : c * 2 * DEPTH + (r + 1) * 16] = (
                    outer[r * 16 : (r + 1) * 16] * keep
                )
        summed = dot_nn(masked[...], hit[...])
        parts = []
        for c in range(group):
            total = summed[c * 2 * DEPTH : c * 2 * DEPTH + DEPTH] + summed[c * 2 * DEPTH + DEPTH : (c + 1) * 2 * DEPTH]
            parts += [total[:, :CY] * sigma, total[:, CY:] * sigma]
        passed = y_filter(jnp.concatenate(parts, axis=0), mat_ref)
        turn = pltpu.roll(both, lax.rem(LANES - n * 2 * group, LANES), 1)
        for h in range(2 * group):
            x = n * 2 * group + h
            part = passed[h * DEPTH : (h + 1) * DEPTH]
            part = part + turn[:, h : h + 1] * edge_fore + turn[:, CX + h : CX + h + 1] * edge_back
            run = part + jnp.where(x == 0, 0.0, x_flat[first + x]) * run
            scaled[x] = x_flat[2 * length + first + x] * run
        return run

    lax.fori_loop(0, CX // (2 * group), step, jnp.zeros((DEPTH, LANES), F32))
    back = jnp.zeros((DEPTH, LANES), F32)
    for x in reversed(range(CX)):
        back = scaled[x] if x == CX - 1 else scaled[x] + x_flat[length + first + x] * back
        out_ref[pl.ds(x, DEPTH, stride=CX), :] = x_flat[2 * length + first + x] * back


def line_kernel(tab, ends_ref, edge_ref, raw_ref, both_out, sums_out):
    own = lax.axis_index("gy")
    count, rows, _ = ends_ref.shape
    fore = jnp.zeros((rows, LANES), F32)
    for j in range(count - 1):
        fore = jnp.where(j < own, ends_ref[j] + tab[ALPHA_Y + j : ALPHA_Y + j + 1, :] * fore, fore)
    back = jnp.zeros((rows, LANES), F32)
    for j in reversed(range(1, count)):
        back = jnp.where(j > own, ends_ref[j] + tab[BETA_Y + j : BETA_Y + j + 1, :] * back, back)
    mine = ends_ref[own] + tab[pl.ds(ALPHA_Y + own, 1), :] * fore
    back = back + tab[pl.ds(FOLD_Y + own + 1, 1), :] * mine
    lane = iota((DEPTH, LANES), 1)
    parts = []
    for q in range(4):
        left = fore if q == 0 else pltpu.roll(fore, LANES - q * CX, 1)
        right = back if q == 1 else pltpu.roll(back, (LANES - q * CX + CX) % LANES, 1)
        parts.append(jnp.where(lane[:rows] < CX, left, right))
    both = jnp.concatenate(parts, axis=0)
    both_out[...] = both
    edge_fore = edge_ref[0:1]
    edge_back = edge_ref[1:2]
    rows = DEPTH // NEAR
    for c in range(2):
        weighted = both * edge_ref[2 + c : 3 + c]
        fore_part = jnp.sum(jnp.where(lane < CX, weighted, 0.0), axis=1, keepdims=True)
        back_part = jnp.sum(jnp.where((lane >= CX) & (lane < 2 * CX), weighted, 0.0), axis=1, keepdims=True)
        total = raw_ref[c] + fore_part * edge_fore + back_part * edge_back
        for k in range(NEAR):
            sums_out[k, c * rows : (c + 1) * rows] = total[k * rows : (k + 1) * rows]


def chain_kernel(block_tab, out):
    zero, one = jnp.float32(0.0), jnp.float32(1.0)

    def put(row, value):
        out[row : row + 1, :] = jnp.full((1, LANES), value, F32)

    for i in range(NX_BLOCKS):
        put(ALPHA_X + i, block_tab[0, i])
        put(BETA_X + i, block_tab[1, i])
        put(GAMMA_X + i, block_tab[2, i])
    fold = zero
    put(FOLD_G + NX_GROUPS, fold)
    for g in reversed(range(NX_GROUPS)):
        entries = [one]
        for k in range(NEAR):
            entries.append(entries[-1] * block_tab[0, g * NEAR + k])
        gamma, beta = zero, one
        for k in reversed(range(NEAR)):
            step = block_tab[1, g * NEAR + k]
            gamma = block_tab[2, g * NEAR + k] * entries[k] + step * gamma
            beta = beta * step
        put(ALPHA_G + g, entries[NEAR])
        put(BETA_G + g, beta)
        put(TURN_G + g, beta * fold)
        fold = gamma + beta * entries[NEAR] * fold
        put(FOLD_G + g, fold)
    fold = zero
    put(FOLD_Y + NY_BLOCKS, fold)
    for j in reversed(range(NY_BLOCKS)):
        alpha, beta = block_tab[3, j], block_tab[4, j]
        put(ALPHA_Y + j, alpha)
        put(BETA_Y + j, beta)
        put(TURN_Y + j, beta * fold)
        fold = block_tab[5, j] + beta * alpha * fold
        put(FOLD_Y + j, fold)


def join_kernel(tab, sums_ref, joined_out):
    own = lax.axis_index("gx") // NEAR
    start = own * NEAR
    rows = sums_ref.shape[1] // 2
    fore = jnp.zeros((rows, LANES), F32)
    fores = []
    for k in range(NEAR):
        fores.append(fore)
        fore = sums_ref[k, :rows] + tab[pl.ds(ALPHA_X + start + k, 1), :] * fore
    back = jnp.zeros((rows, LANES), F32)
    for k in reversed(range(NEAR)):
        back = (
            sums_ref[k, rows:]
            + tab[pl.ds(GAMMA_X + start + k, 1), :] * fores[k]
            + tab[pl.ds(BETA_X + start + k, 1), :] * back
        )
    back = back + tab[pl.ds(TURN_G + own, 1), :] * fore
    for g in range(joined_out.shape[0]):
        joined_out[g] = jnp.where(own <= g, fore, back)


def carry_kernel(tab, joined_ref, sums_ref, carry_out):
    own = lax.axis_index("gx") // NEAR
    start = own * NEAR
    groups, rows, _ = joined_ref.shape
    fore = jnp.zeros((rows, LANES), F32)
    for g in range(groups - 1):
        fore = jnp.where(g < own, joined_ref[g] + tab[ALPHA_G + g : ALPHA_G + g + 1, :] * fore, fore)
    back = jnp.zeros((rows, LANES), F32)
    for g in reversed(range(1, groups)):
        back = jnp.where(g > own, joined_ref[g] + tab[BETA_G + g : BETA_G + g + 1, :] * back, back)
    mine = joined_ref[own] + tab[pl.ds(ALPHA_G + own, 1), :] * fore
    back = back + tab[pl.ds(FOLD_G + own + 1, 1), :] * mine
    fores = []
    for k in range(NEAR):
        carry_out[k, :rows] = fore
        fores.append(fore)
        fore = sums_ref[k, :rows] + tab[pl.ds(ALPHA_X + start + k, 1), :] * fore
    for k in reversed(range(NEAR)):
        carry_out[k, rows:] = back
        back = (
            sums_ref[k, rows:]
            + tab[pl.ds(GAMMA_X + start + k, 1), :] * fores[k]
            + tab[pl.ds(BETA_X + start + k, 1), :] * back
        )


def final_kernel(carry_ref, ends_ref, block_ref, out_ref):
    rows = carry_ref.shape[1] // 2
    fore = ends_ref[:CX]
    back = ends_ref[CX:]
    base = pl.program_id(0) * (rows * CX)
    for r in range(rows):
        out_ref[r * CX : (r + 1) * CX] = (
            block_ref[pl.ds(pl.multiple_of(base + r * CX, CX), CX), :]
            + carry_ref[0, r : r + 1] * fore
            + carry_ref[0, rows + r : rows + r + 1] * back
        )


def table(gap):
    decay = 1.0 - gap
    edge = jnp.zeros((1,), F32)
    prior = jnp.concatenate([edge, decay[:-1]])
    later = jnp.concatenate([decay[1:], edge])
    return jnp.stack([prior, later, jnp.sqrt(gap * (2.0 - gap))])


def call(kernel, outs, specs, scratch=(), mib=48):
    shapes = tuple(jax.ShapeDtypeStruct(s, t) for s, t in outs)
    return pl.pallas_call(
        kernel,
        out_shape=shapes if len(shapes) > 1 else shapes[0],
        in_specs=specs,
        out_specs=(vmem,) * len(shapes) if len(shapes) > 1 else vmem,
        scratch_shapes=scratch,
        compiler_params=params(mib),
    )


def local(bin_resid, geometry, beam_weight, dest_device, dest_column, live_count, field_sigma, x_gap, y_gap):
    count_x = lax.axis_size("gx")
    count_y = lax.axis_size("gy")
    peers = count_x * count_y
    bins = bin_resid.shape[0]
    slots = SLOTS * peers
    far = count_x // NEAR
    chunk = 2 * DEPTH // NEAR
    near_groups = [[g * NEAR + k for k in range(NEAR)] for g in range(far)]
    far_groups = [[g * NEAR + k for g in range(far)] for k in range(NEAR)]
    side_groups = [[i * count_y + j for i in group for j in range(count_y)] for group in near_groups]
    a2a = functools.partial(lax.all_to_all, tiled=True)
    tie = lax.optimization_barrier

    row = (1, bins)
    send = call(
        pack_kernel,
        [((peers, SLOTS * WIDTH), F32)],
        [smem] + [hbm] * 5,
        [
            pltpu.VMEM(row, F32),
            pltpu.VMEM(row, I32),
            pltpu.VMEM(row, I32),
            pltpu.VMEM((FIELDS, bins), F32),
            pltpu.VMEM((LEVELS, bins), F32),
            pltpu.SemaphoreType.DMA((5,)),
        ],
        60,
    )(
        live_count,
        bin_resid.reshape(row),
        dest_device.reshape(row),
        dest_column.reshape(row),
        geometry,
        beam_weight,
    )
    moved = a2a(send.reshape(far, peers // far, SLOTS * WIDTH), "gx", split_axis=0, concat_axis=0, axis_index_groups=far_groups)
    tab_x = table(x_gap)
    tab_y = table(y_gap)
    x_flat = tab_x.reshape(-1)
    sigma = jnp.broadcast_to(field_sigma.reshape(DEPTH, 1), (DEPTH, LANES))
    coefs = call(
        coef_kernel,
        [
            ((2 * CY, 2 * CY), BF16),
            ((4, CY, LANES), F32),
            ((8, LANES), F32),
            ((8, LANES), F32),
            ((2 * CX, LANES), F32),
        ],
        [smem, smem, vmem, vmem, vmem],
        [pltpu.VMEM((CY, LANES), F32)] * 3,
    )(
        x_flat,
        tab_y.reshape(-1),
        tab_x.reshape(3, count_x, CX).transpose(0, 2, 1),
        tab_y.reshape(3, count_y, CY).transpose(0, 2, 1),
        tab_y.reshape(3, count_y, CY),
    )
    scalars = call(chain_kernel, [((TAB_ROWS, LANES), F32)], [smem])(coefs[3])
    moved, coefs, sigma, scalars = tie((moved, coefs, sigma, scalars))
    mat, tab, edge, _, x_ends = coefs
    moved = a2a(moved.transpose(1, 0, 2), ("gx", "gy"), split_axis=0, concat_axis=0, axis_index_groups=side_groups)
    moved = moved.reshape(peers, SLOTS * WIDTH)
    weighted = pltpu.VMEM((4 * DEPTH, slots), BF16)
    turned, ends = call(
        ends_kernel,
        [((SLOTS * WIDTH, peers), F32), ((count_y, DEPTH // 4, LANES), F32)],
        [vmem] * 4,
        [weighted],
    )(moved, sigma, tab, scalars)
    ends = a2a(ends, "gy", split_axis=0, concat_axis=0)
    raw = call(sums_kernel, [((2, DEPTH, LANES), F32)], [vmem] * 4, [weighted])(turned, sigma, tab, mat)
    both, sums = call(
        line_kernel,
        [((DEPTH, LANES), F32), ((NEAR, chunk, LANES), F32)],
        [vmem] * 4,
    )(scalars, ends, edge, raw)
    sums = a2a(sums, "gx", split_axis=0, concat_axis=0, axis_index_groups=near_groups)
    joined = call(join_kernel, [((far, chunk // 2, LANES), F32)], [vmem, vmem])(scalars, sums)
    joined, both = tie((joined, both))
    joined = a2a(joined, "gx", split_axis=0, concat_axis=0, axis_index_groups=far_groups)
    block = call(
        grid_kernel,
        [((DEPTH * CX, LANES), F32)],
        [smem] + [vmem] * 6,
        [
            pltpu.VMEM((2 * DEPTH, slots), BF16),
            pltpu.VMEM((8 * DEPTH, slots), BF16),
            pltpu.VMEM((slots, 2 * CY), BF16),
            pltpu.VMEM((CX, DEPTH, LANES), F32),
        ],
    )(x_flat, turned, moved, sigma, mat, both, edge)
    joined, block = tie((joined, block))
    carry = call(carry_kernel, [((NEAR, chunk, LANES), F32)], [vmem] * 3)(scalars, joined, sums)
    carry = a2a(carry, "gx", split_axis=0, concat_axis=0, axis_index_groups=near_groups)
    rows = DEPTH * CX // NEAR
    out = pl.pallas_call(
        final_kernel,
        grid=(NEAR,),
        out_shape=jax.ShapeDtypeStruct((DEPTH * CX, LANES), F32),
        in_specs=[pl.BlockSpec((1, chunk, LANES), lambda k: (k, 0, 0)), vmem, vmem],
        out_specs=pl.BlockSpec((rows, LANES), lambda k: (k, 0)),
        compiler_params=params(),
    )(carry, x_ends, block)
    return out.reshape(FIELDS, LEVELS, CX, CY)


def solution(mesh):
    both = ("gx", "gy")
    placed = (P(both), P(None, both), P(None, both), P(both, None), P(both), P(both), P(), P(), P())
    return jax.shard_map(
        local, mesh=mesh, in_specs=placed, out_specs=P(None, None, "gx", "gy"), check_vma=False
    )
```

```python
import functools
import jax
import jax.numpy as jnp
from jax import lax
from jax.experimental import pallas as pl
from jax.experimental.pallas import tpu as pltpu
from jax.sharding import PartitionSpec as P

F32 = jnp.float32
BF16 = jnp.bfloat16
I32 = jnp.int32
LANES = 128
FIELDS = 6
LEVELS = 16
DEPTH = FIELDS * LEVELS
SLOTS = 4
WIDTH = 24
CX = 32
CY = 128
NEAR = 4
GROUP = 4
EARLY = 1
NX_GROUPS = 8
NX_BLOCKS = NX_GROUPS * NEAR
NY_BLOCKS = 16
ALPHA_X, BETA_X, GAMMA_X = 0, 32, 64
ALPHA_Y, BETA_Y, FOLD_Y, TURN_Y = 96, 112, 128, 152
ALPHA_G, BETA_G, FOLD_G, TURN_G = 168, 176, 184, 200
TAB_ROWS = 208


def params(mib=48):
    return pltpu.CompilerParams(vmem_limit_bytes=mib * 1024 * 1024)


vmem = pl.BlockSpec(memory_space=pltpu.VMEM)
smem = pl.BlockSpec(memory_space=pltpu.SMEM)
hbm = pl.BlockSpec(memory_space=pltpu.HBM)


def iota(shape, dim):
    return lax.broadcasted_iota(I32, shape, dim)


def split_two(values):
    high = values.astype(BF16)
    return high, (values - high.astype(F32)).astype(BF16)


def dot_nt(left, right):
    return lax.dot_general(left, right, (((1,), (1,)), ((), ())), preferred_element_type=F32)


def dot_nn(left, right):
    return lax.dot_general(left, right, (((1,), (0,)), ((), ())), preferred_element_type=F32)


def pack_kernel(live_ref, *refs):
    sources, (send_ref, *buffers, sems) = refs[:5], refs[5:]
    copies = [pltpu.make_async_copy(src, buf, sems.at[k]) for k, (src, buf) in enumerate(zip(sources, buffers))]
    for copy in copies:
        copy.start()
    for copy in copies:
        copy.wait()
    resid_ref, dest_ref, column_ref, geometry_ref, beam_ref = buffers
    bins = resid_ref.shape[1]
    peers = send_ref.shape[0]
    dest = dest_ref[...]
    dest_f = dest.astype(F32)
    dest_t = jnp.broadcast_to(dest_f, (LANES, bins)).T
    ranks = []
    for chunk in range(bins // LANES):
        rows = (chunk + 1) * LANES
        same = dest_t[:rows] == dest_f[:, chunk * LANES : rows]
        before = iota((rows, LANES), 0) < iota((rows, LANES), 1) + chunk * LANES
        ranks.append(jnp.sum(jnp.where(same & before, 1.0, 0.0), axis=0, keepdims=True))
    rank = jnp.concatenate(ranks, axis=1)
    alive = jnp.where(iota((1, bins), 1) < live_ref[0], 1.0, 0.0)
    weighted = geometry_ref[...] * (alive * resid_ref[...])
    payload = jnp.concatenate(
        [
            beam_ref[...],
            weighted,
            column_ref[...].astype(F32),
            jnp.zeros((WIDTH - LEVELS - FIELDS - 1, bins), F32),
        ],
        axis=0,
    )
    spread = jnp.concatenate([jnp.where(rank == float(s), payload, 0.0) for s in range(SLOTS)], axis=0)
    high, low = split_two(spread)
    onehot = jnp.where(iota((peers, bins), 0) == dest, 1.0, 0.0).astype(BF16)
    both = dot_nt(onehot, jnp.concatenate([high, low], axis=0))
    send_ref[...] = both[:, : SLOTS * WIDTH] + both[:, SLOTS * WIDTH :]


def coef_kernel(x_flat, y_flat, x_cols, y_cols, y_rows, mat_ref, tab_ref, edge_ref, block_ref, ends_ref, chain, gammas, betas):
    own_x = lax.axis_index("gx")
    own_y = lax.axis_index("gy")
    length = y_rows.shape[1] * LANES
    span = x_cols.shape[2] * CX

    def block_scalars(cols, row):
        steps, blocks = cols.shape[1:]

        def forward(p, value):
            value = value * cols[0, pl.ds(p, 1), :]
            gammas[pl.ds(p, 1), :blocks] = value
            return value

        alpha = lax.fori_loop(0, steps, forward, jnp.ones((1, blocks), F32))

        def backward(k, carried):
            gamma, beta = carried
            p = steps - 1 - k
            later = cols[1, pl.ds(p, 1), :]
            gamma = cols[2, pl.ds(p, 1), :] * gammas[pl.ds(p, 1), :blocks] + later * gamma
            beta = beta * later
            gammas[pl.ds(p, 1), :blocks] = gamma
            betas[pl.ds(p, 1), :blocks] = beta
            return gamma, beta

        gamma, beta = lax.fori_loop(
            0, steps, backward, (jnp.zeros((1, blocks), F32), jnp.ones((1, blocks), F32))
        )
        block_ref[row : row + 1, :blocks] = alpha
        block_ref[row + 1 : row + 2, :blocks] = beta
        block_ref[row + 2 : row + 3, :blocks] = gamma

    block_ref[...] = jnp.zeros(block_ref.shape, F32)
    block_scalars(y_cols, 3)
    block_scalars(x_cols, 0)
    blocks = x_cols.shape[2]
    mine = iota((CX, blocks), 1) == own_x
    for k, scratch in enumerate((gammas, betas)):
        picked = jnp.where(mine, scratch[:CX, :blocks] * x_cols[2], 0.0)
        ends_ref[k * CX : (k + 1) * CX] = jnp.broadcast_to(
            jnp.sum(picked, axis=1, keepdims=True), (CX, LANES)
        )

    lane = iota((1, LANES), 1)
    first = own_x * CX
    down = []
    weight = jnp.float32(1.0)
    for x in range(CX):
        down.append(weight * x_flat[2 * span + first + x])
        weight = weight * x_flat[span + first + x]
    tail, start = jnp.float32(1.0), down[CX - 1]
    tails, starts = [tail], [start]
    for x in reversed(range(CX - 1)):
        factor = x_flat[first + x + 1]
        tail = tail * factor
        start = down[x] + factor * start
        tails.append(tail)
        starts.append(start)
    row_tail = jnp.zeros((1, LANES), F32)
    row_start = jnp.zeros((1, LANES), F32)
    for x in range(CX):
        row_tail = jnp.where(lane % CX == x, tails[CX - 1 - x], row_tail)
        row_start = jnp.where(lane % CX == x, starts[CX - 1 - x], row_start)

    first = own_y * CY

    def fill(n, row):
        row = jnp.where(lane == n, 1.0, row * y_flat[first + n])
        chain[pl.ds(n, 1), :] = row
        return row

    lax.fori_loop(0, CY, fill, jnp.zeros((1, LANES), F32))

    def unfill(k, row):
        n = CY - 1 - k
        row = chain[pl.ds(n, 1), :] * y_flat[2 * length + first + n] + row * y_flat[length + first + n]
        chain[pl.ds(n, 1), :] = row
        return row

    lax.fori_loop(0, CY, unfill, jnp.zeros((1, LANES), F32))
    scale = y_rows[2, pl.ds(own_y, 1), :]
    filt = chain[...].T * scale
    high, low = split_two(filt)
    mat_ref[:CY, :CY] = high
    mat_ref[:CY, CY:] = low
    mat_ref[CY:, :CY] = high
    mat_ref[CY:, CY:] = jnp.zeros((CY, CY), BF16)
    scale_first = scale[:, :1]
    scale_last = scale[:, CY - 1 :]
    tab_ref[0] = jnp.broadcast_to(filt[:, CY - 1 :] / (scale_last * scale_last), (CY, LANES))
    tab_ref[1] = jnp.broadcast_to(filt[:, :1] / scale_first, (CY, LANES))
    edge_ref[...] = jnp.zeros(edge_ref.shape, F32)
    edge_ref[0:1] = filt[:1] * y_flat[first]
    edge_ref[1:2] = filt[CY - 1 :] * y_flat[length + first + CY - 1] / scale_last
    edge_ref[2:3] = row_tail
    edge_ref[3:4] = row_start
    for c, row in enumerate((row_tail, row_start)):
        tab_ref[2 + c] = jnp.broadcast_to(jnp.where(lane < CX, row, 0.0), (LANES, LANES)).T


def on_lines(turned, s):
    row = s * WIDTH + LEVELS + FIELDS
    place = turned[row : row + 1].astype(I32)
    on_y = iota((CY, place.shape[1]), 0) == (place & (CY - 1))
    on_x = iota((CX, place.shape[1]), 0) == (place >> 7)
    return on_x, on_y


def weighted_hits(on_line, on_cross, columns):
    rows = []
    for column in columns:
        weight = jnp.sum(jnp.where(on_cross, column, 0.0), axis=0, keepdims=True)
        rows += list(split_two(jnp.where(on_line, weight, 0.0)))
    return jnp.concatenate(rows, axis=0)


def ends_kernel(recv_ref, sigma_ref, tab_ref, scalars, turned_out, outer_out, ends_out):
    sources = recv_ref.shape[0]
    turned = recv_ref[...].T
    turned_out[...] = turned
    columns = [jnp.concatenate([tab_ref[c]] * (sources // LANES), axis=1) for c in range(2)]
    hits = []
    for s in range(SLOTS):
        at = slice(s * sources, (s + 1) * sources)
        base = s * WIDTH
        on_x, on_y = on_lines(turned, s)
        hits.append(weighted_hits(on_x, on_y, columns))
        for f in range(FIELDS):
            high, low = split_two(
                turned[base : base + LEVELS] * turned[base + LEVELS + f : base + LEVELS + f + 1]
            )
            outer_out[f * LEVELS : (f + 1) * LEVELS, at] = high
            outer_out[DEPTH + f * LEVELS : DEPTH + (f + 1) * LEVELS, at] = low
    summed = dot_nt(outer_out[...], jnp.concatenate(hits, axis=1))
    summed = (summed[:DEPTH] + summed[DEPTH:]) * sigma_ref[...]
    summed = summed + pltpu.roll(summed, LANES - CX, 1)
    own = lax.axis_index("gy")
    folded = pltpu.roll(summed, 64, 1) + scalars[pl.ds(TURN_Y + own, 1), :] * summed
    rows = DEPTH // 4
    quarter = iota((rows, LANES), 1) // CX
    fore_row, back_row = summed[:rows], folded[:rows]
    for q in range(1, 4):
        at = slice(q * rows, (q + 1) * rows)
        fore_row = jnp.where(quarter == q, pltpu.roll(summed[at], q * CX, 1), fore_row)
        back_row = jnp.where(quarter == q, pltpu.roll(folded[at], q * CX, 1), back_row)
    for j in range(ends_out.shape[0]):
        ends_out[j] = jnp.where(own <= j, fore_row, back_row)


def y_filter(values, mat_ref):
    passed = dot_nn(jnp.concatenate(split_two(values), axis=1), mat_ref[...])
    return passed[:, :CY] + passed[:, CY:]


def place_steps(begin, end, pair, outer, hit, sigma, mat_ref, masked, emit):
    def step(n, carried):
        for c in range(GROUP):
            keep = jnp.where(pair == n * GROUP + c, 1.0, 0.0)
            keep = jnp.broadcast_to(keep, (16, keep.shape[1])).astype(BF16)
            for r in range(2 * DEPTH // 16):
                masked[c * 2 * DEPTH + r * 16 : c * 2 * DEPTH + (r + 1) * 16] = (
                    outer[r * 16 : (r + 1) * 16] * keep
                )
        summed = dot_nn(masked[...], hit[...])
        parts = []
        for c in range(GROUP):
            base = c * 2 * DEPTH
            total = summed[base : base + DEPTH] + summed[base + DEPTH : base + 2 * DEPTH]
            parts += [total[:, :CY] * sigma, total[:, CY:] * sigma]
        passed = y_filter(jnp.concatenate(parts, axis=0), mat_ref)
        return emit(n, passed, carried)

    return functools.partial(lax.fori_loop, begin, end, step)


def pairs_of(turned_ref):
    rows = [turned_ref[s * WIDTH + LEVELS + FIELDS : s * WIDTH + LEVELS + FIELDS + 1] for s in range(SLOTS)]
    return jnp.concatenate(rows, axis=1).astype(I32) >> 8


def early_kernel(turned_ref, outer, recv_ref, sigma_ref, tab_ref, mat_ref, sums_out, hit, block_out, masked):
    turned = turned_ref[...]
    sources = turned.shape[1]
    sigma = sigma_ref[...]
    columns = [jnp.concatenate([tab_ref[2 + c, :CX]] * (sources // LANES), axis=1) for c in range(2)]
    hits = []
    for s in range(SLOTS):
        on_x, on_y = on_lines(turned, s)
        hits.append(weighted_hits(on_y, on_x, columns))
    summed = dot_nt(outer[...], jnp.concatenate(hits, axis=1))
    summed = summed[:DEPTH] + summed[DEPTH:]
    both = [(summed[:, k : k + CY] + summed[:, k + CY : k + 2 * CY]) * sigma for k in (0, 2 * CY)]
    both = y_filter(jnp.concatenate(both, axis=0), mat_ref)
    sums_out[0] = both[:DEPTH]
    sums_out[1] = both[DEPTH:]

    lane2 = iota((1, 2 * LANES), 1)
    for s in range(SLOTS):
        place = s * WIDTH + LEVELS + FIELDS
        cols = jnp.broadcast_to(recv_ref[:, place : place + 1], (sources, LANES)).astype(I32) & (2 * CY - 1)
        cols = jnp.concatenate([cols, cols], axis=1)
        hit[s * sources : (s + 1) * sources] = jnp.where(cols == lane2, 1.0, 0.0).astype(BF16)

    def emit(n, passed, carried):
        for h in range(2 * GROUP):
            block_out[n * 2 * GROUP + h] = passed[h * DEPTH : (h + 1) * DEPTH]
        return carried

    place_steps(0, EARLY, pairs_of(turned_ref), outer, hit, sigma, mat_ref, masked, emit)(0)


def grid_kernel(x_flat, turned_ref, outer, hit, block_ref, sigma_ref, mat_ref, both_ref, edge_ref, out_ref, masked, scaled):
    first = lax.axis_index("gx") * CX
    length = x_flat.shape[0] // 3
    both = both_ref[...]
    edge_fore = edge_ref[0:1]
    edge_back = edge_ref[1:2]

    def advance(x, part, fore, back, run):
        part = part + fore * edge_fore + back * edge_back
        run = part + jnp.where(x == 0, 0.0, x_flat[first + x]) * run
        scaled[x] = x_flat[2 * length + first + x] * run
        return run

    run = jnp.zeros((DEPTH, LANES), F32)
    for x in range(EARLY * 2 * GROUP):
        run = advance(x, block_ref[x], both[:, x : x + 1], both[:, CX + x : CX + x + 1], run)

    def emit(n, passed, run):
        turn = pltpu.roll(both, lax.rem(LANES - n * 2 * GROUP, LANES), 1)
        for h in range(2 * GROUP):
            part = passed[h * DEPTH : (h + 1) * DEPTH]
            run = advance(n * 2 * GROUP + h, part, turn[:, h : h + 1], turn[:, CX + h : CX + h + 1], run)
        return run

    steps = CX // (2 * GROUP)
    place_steps(EARLY, steps, pairs_of(turned_ref), outer, hit, sigma_ref[...], mat_ref, masked, emit)(run)
    back = jnp.zeros((DEPTH, LANES), F32)
    for x in reversed(range(CX)):
        back = scaled[x] if x == CX - 1 else scaled[x] + x_flat[length + first + x] * back
        out_ref[pl.ds(x, DEPTH, stride=CX), :] = x_flat[2 * length + first + x] * back


def line_kernel(tab, ends_ref, edge_ref, raw_ref, both_out, sums_out):
    own = lax.axis_index("gy")
    count, rows, _ = ends_ref.shape
    fore = jnp.zeros((rows, LANES), F32)
    for j in range(count - 1):
        fore = jnp.where(j < own, ends_ref[j] + tab[ALPHA_Y + j : ALPHA_Y + j + 1, :] * fore, fore)
    back = jnp.zeros((rows, LANES), F32)
    for j in reversed(range(1, count)):
        back = jnp.where(j > own, ends_ref[j] + tab[BETA_Y + j : BETA_Y + j + 1, :] * back, back)
    mine = ends_ref[own] + tab[pl.ds(ALPHA_Y + own, 1), :] * fore
    back = back + tab[pl.ds(FOLD_Y + own + 1, 1), :] * mine
    lane = iota((DEPTH, LANES), 1)
    parts = []
    for q in range(4):
        left = fore if q == 0 else pltpu.roll(fore, LANES - q * CX, 1)
        right = back if q == 1 else pltpu.roll(back, (LANES - q * CX + CX) % LANES, 1)
        parts.append(jnp.where(lane[:rows] < CX, left, right))
    both = jnp.concatenate(parts, axis=0)
    both_out[...] = both
    edge_fore = edge_ref[0:1]
    edge_back = edge_ref[1:2]
    rows = DEPTH // NEAR
    for c in range(2):
        weighted = both * edge_ref[2 + c : 3 + c]
        fore_part = jnp.sum(jnp.where(lane < CX, weighted, 0.0), axis=1, keepdims=True)
        back_part = jnp.sum(jnp.where((lane >= CX) & (lane < 2 * CX), weighted, 0.0), axis=1, keepdims=True)
        total = raw_ref[c] + fore_part * edge_fore + back_part * edge_back
        for k in range(NEAR):
            sums_out[k, c * rows : (c + 1) * rows] = total[k * rows : (k + 1) * rows]


def chain_kernel(block_tab, out):
    zero, one = jnp.float32(0.0), jnp.float32(1.0)

    def put(row, value):
        out[row : row + 1, :] = jnp.full((1, LANES), value, F32)

    for i in range(NX_BLOCKS):
        put(ALPHA_X + i, block_tab[0, i])
        put(BETA_X + i, block_tab[1, i])
        put(GAMMA_X + i, block_tab[2, i])
    fold = zero
    put(FOLD_G + NX_GROUPS, fold)
    for g in reversed(range(NX_GROUPS)):
        entries = [one]
        for k in range(NEAR):
            entries.append(entries[-1] * block_tab[0, g * NEAR + k])
        gamma, beta = zero, one
        for k in reversed(range(NEAR)):
            step = block_tab[1, g * NEAR + k]
            gamma = block_tab[2, g * NEAR + k] * entries[k] + step * gamma
            beta = beta * step
        put(ALPHA_G + g, entries[NEAR])
        put(BETA_G + g, beta)
        put(TURN_G + g, beta * fold)
        fold = gamma + beta * entries[NEAR] * fold
        put(FOLD_G + g, fold)
    fold = zero
    put(FOLD_Y + NY_BLOCKS, fold)
    for j in reversed(range(NY_BLOCKS)):
        alpha, beta = block_tab[3, j], block_tab[4, j]
        put(ALPHA_Y + j, alpha)
        put(BETA_Y + j, beta)
        put(TURN_Y + j, beta * fold)
        fold = block_tab[5, j] + beta * alpha * fold
        put(FOLD_Y + j, fold)


def join_kernel(tab, sums_ref, joined_out):
    own = lax.axis_index("gx") // NEAR
    start = own * NEAR
    rows = sums_ref.shape[1] // 2
    fore = jnp.zeros((rows, LANES), F32)
    fores = []
    for k in range(NEAR):
        fores.append(fore)
        fore = sums_ref[k, :rows] + tab[pl.ds(ALPHA_X + start + k, 1), :] * fore
    back = jnp.zeros((rows, LANES), F32)
    for k in reversed(range(NEAR)):
        back = (
            sums_ref[k, rows:]
            + tab[pl.ds(GAMMA_X + start + k, 1), :] * fores[k]
            + tab[pl.ds(BETA_X + start + k, 1), :] * back
        )
    back = back + tab[pl.ds(TURN_G + own, 1), :] * fore
    for g in range(joined_out.shape[0]):
        joined_out[g] = jnp.where(own <= g, fore, back)


def carry_kernel(tab, joined_ref, sums_ref, carry_out):
    own = lax.axis_index("gx") // NEAR
    start = own * NEAR
    groups, rows, _ = joined_ref.shape
    fore = jnp.zeros((rows, LANES), F32)
    for g in range(groups - 1):
        fore = jnp.where(g < own, joined_ref[g] + tab[ALPHA_G + g : ALPHA_G + g + 1, :] * fore, fore)
    back = jnp.zeros((rows, LANES), F32)
    for g in reversed(range(1, groups)):
        back = jnp.where(g > own, joined_ref[g] + tab[BETA_G + g : BETA_G + g + 1, :] * back, back)
    mine = joined_ref[own] + tab[pl.ds(ALPHA_G + own, 1), :] * fore
    back = back + tab[pl.ds(FOLD_G + own + 1, 1), :] * mine
    fores = []
    for k in range(NEAR):
        carry_out[k, :rows] = fore
        fores.append(fore)
        fore = sums_ref[k, :rows] + tab[pl.ds(ALPHA_X + start + k, 1), :] * fore
    for k in reversed(range(NEAR)):
        carry_out[k, rows:] = back
        back = (
            sums_ref[k, rows:]
            + tab[pl.ds(GAMMA_X + start + k, 1), :] * fores[k]
            + tab[pl.ds(BETA_X + start + k, 1), :] * back
        )


def final_kernel(carry_ref, ends_ref, block_ref, out_ref):
    rows = carry_ref.shape[1] // 2
    fore = ends_ref[:CX]
    back = ends_ref[CX:]
    step = pl.program_id(0)
    base = step * (rows * CX)
    for r in range(rows):
        out_ref[r * CX : (r + 1) * CX] = (
            block_ref[pl.ds(pl.multiple_of(base + r * CX, CX), CX), :]
            + carry_ref[step, r : r + 1] * fore
            + carry_ref[step, rows + r : rows + r + 1] * back
        )


def table(gap):
    decay = 1.0 - gap
    edge = jnp.zeros((1,), F32)
    prior = jnp.concatenate([edge, decay[:-1]])
    later = jnp.concatenate([decay[1:], edge])
    return jnp.stack([prior, later, jnp.sqrt(gap * (2.0 - gap))])


def call(kernel, outs, specs, scratch=(), mib=48):
    shapes = tuple(jax.ShapeDtypeStruct(s, t) for s, t in outs)
    return pl.pallas_call(
        kernel,
        out_shape=shapes if len(shapes) > 1 else shapes[0],
        in_specs=specs,
        out_specs=(vmem,) * len(shapes) if len(shapes) > 1 else vmem,
        scratch_shapes=scratch,
        compiler_params=params(mib),
    )


def local(bin_resid, geometry, beam_weight, dest_device, dest_column, live_count, field_sigma, x_gap, y_gap):
    count_x = lax.axis_size("gx")
    count_y = lax.axis_size("gy")
    peers = count_x * count_y
    bins = bin_resid.shape[0]
    slots = SLOTS * peers
    far = count_x // NEAR
    chunk = 2 * DEPTH // NEAR
    near_groups = [[g * NEAR + k for k in range(NEAR)] for g in range(far)]
    far_groups = [[g * NEAR + k for g in range(far)] for k in range(NEAR)]
    side_groups = [[i * count_y + j for i in group for j in range(count_y)] for group in near_groups]
    a2a = functools.partial(lax.all_to_all, tiled=True)
    tie = lax.optimization_barrier

    row = (1, bins)
    moved = call(
        pack_kernel,
        [((peers, SLOTS * WIDTH), F32)],
        [smem] + [hbm] * 5,
        [
            pltpu.VMEM(row, F32),
            pltpu.VMEM(row, I32),
            pltpu.VMEM(row, I32),
            pltpu.VMEM((FIELDS, bins), F32),
            pltpu.VMEM((LEVELS, bins), F32),
            pltpu.SemaphoreType.DMA((5,)),
        ],
        60,
    )(
        live_count,
        bin_resid.reshape(row),
        dest_device.reshape(row),
        dest_column.reshape(row),
        geometry,
        beam_weight,
    )
    tab_x = table(x_gap)
    tab_y = table(y_gap)
    x_flat = tab_x.reshape(-1)
    sigma = jnp.broadcast_to(field_sigma.reshape(DEPTH, 1), (DEPTH, LANES))
    coefs = call(
        coef_kernel,
        [
            ((2 * CY, 2 * CY), BF16),
            ((4, CY, LANES), F32),
            ((8, LANES), F32),
            ((8, LANES), F32),
            ((2 * CX, LANES), F32),
        ],
        [smem, smem, vmem, vmem, vmem],
        [pltpu.VMEM((CY, LANES), F32)] * 3,
    )(
        x_flat,
        tab_y.reshape(-1),
        tab_x.reshape(3, count_x, CX).transpose(0, 2, 1),
        tab_y.reshape(3, count_y, CY).transpose(0, 2, 1),
        tab_y.reshape(3, count_y, CY),
    )
    scalars = call(chain_kernel, [((TAB_ROWS, LANES), F32)], [smem])(coefs[3])
    mat, tab, edge, _, x_ends = coefs
    moved = a2a(moved.reshape(peers, 1, SLOTS * WIDTH), ("gx", "gy"), split_axis=0, concat_axis=0)
    moved, coefs, sigma, scalars = tie((moved, coefs, sigma, scalars))
    moved = moved.reshape(peers, SLOTS * WIDTH)
    turned, outer, ends = call(
        ends_kernel,
        [((SLOTS * WIDTH, peers), F32), ((2 * DEPTH, slots), BF16), ((count_y, DEPTH // 4, LANES), F32)],
        [vmem] * 4,
    )(moved, sigma, tab, scalars)
    ends = a2a(ends, "gy", split_axis=0, concat_axis=0)
    masked = pltpu.VMEM((GROUP * 2 * DEPTH, slots), BF16)
    raw, hit, block = call(
        early_kernel,
        [
            ((2, DEPTH, LANES), F32),
            ((slots, 2 * CY), BF16),
            ((EARLY * 2 * GROUP, DEPTH, LANES), F32),
        ],
        [vmem] * 6,
        [masked],
    )(turned, outer, moved, sigma, tab, mat)
    both, sums = call(
        line_kernel,
        [((DEPTH, LANES), F32), ((NEAR, chunk, LANES), F32)],
        [vmem] * 4,
    )(scalars, ends, edge, raw)
    sums = a2a(sums, "gx", split_axis=0, concat_axis=0, axis_index_groups=near_groups)
    joined = call(join_kernel, [((far, chunk // 2, LANES), F32)], [vmem, vmem])(scalars, sums)
    joined, both = tie((joined, both))
    joined = a2a(joined, "gx", split_axis=0, concat_axis=0, axis_index_groups=far_groups)
    block = call(
        grid_kernel,
        [((DEPTH * CX, LANES), F32)],
        [smem] + [vmem] * 8,
        [masked, pltpu.VMEM((CX, DEPTH, LANES), F32)],
    )(x_flat, turned, outer, hit, block, sigma, mat, both, edge)
    joined, block = tie((joined, block))
    carry = call(carry_kernel, [((NEAR, chunk, LANES), F32)], [vmem] * 3)(scalars, joined, sums)
    carry = a2a(carry, "gx", split_axis=0, concat_axis=0, axis_index_groups=near_groups)
    rows = DEPTH * CX // NEAR
    out = pl.pallas_call(
        final_kernel,
        grid=(NEAR,),
        out_shape=jax.ShapeDtypeStruct((DEPTH * CX, LANES), F32),
        in_specs=[vmem] * 3,
        out_specs=pl.BlockSpec((rows, LANES), lambda k: (k, 0)),
        compiler_params=params(),
    )(carry, x_ends, block)
    return out.reshape(FIELDS, LEVELS, CX, CY)


def solution(mesh):
    both = ("gx", "gy")
    placed = (P(both), P(None, both), P(None, both), P(both, None), P(both), P(both), P(), P(), P())
    return jax.shard_map(
        local, mesh=mesh, in_specs=placed, out_specs=P(None, None, "gx", "gy"), check_vma=False
    )
```

```python
import functools
import jax
import jax.numpy as jnp
from jax import lax
from jax.experimental import pallas as pl
from jax.experimental.pallas import tpu as pltpu
from jax.sharding import PartitionSpec as P

F32 = jnp.float32
BF16 = jnp.bfloat16
I32 = jnp.int32
LANES = 128
FIELDS = 6
LEVELS = 16
DEPTH = FIELDS * LEVELS
SLOTS = 4
WIDTH = 24
CX = 32
CY = 128
NEAR = 4
GROUP = 4
FINAL_STEPS = 2
EARLY = 1
NX_GROUPS = 8
NX_BLOCKS = NX_GROUPS * NEAR
NY_BLOCKS = 16
ALPHA_X, BETA_X, GAMMA_X = 0, 32, 64
ALPHA_Y, BETA_Y, FOLD_Y, TURN_Y = 96, 112, 128, 152
ALPHA_G, BETA_G, FOLD_G, TURN_G = 168, 176, 184, 200
TAB_ROWS = 208


def params(mib=48):
    return pltpu.CompilerParams(vmem_limit_bytes=mib * 1024 * 1024)


vmem = pl.BlockSpec(memory_space=pltpu.VMEM)
smem = pl.BlockSpec(memory_space=pltpu.SMEM)
hbm = pl.BlockSpec(memory_space=pltpu.HBM)


def iota(shape, dim):
    return lax.broadcasted_iota(I32, shape, dim)


def split_two(values):
    high = values.astype(BF16)
    return high, (values - high.astype(F32)).astype(BF16)


def dot_nt(left, right):
    return lax.dot_general(left, right, (((1,), (1,)), ((), ())), preferred_element_type=F32)


def dot_nn(left, right):
    return lax.dot_general(left, right, (((1,), (0,)), ((), ())), preferred_element_type=F32)


def pack_kernel(live_ref, *refs):
    sources, (send_ref, *buffers, sems) = refs[:5], refs[5:]
    copies = [pltpu.make_async_copy(src, buf, sems.at[k]) for k, (src, buf) in enumerate(zip(sources, buffers))]
    for k in (1, 0, 2, 3, 4):
        copies[k].start()
    copies[1].wait()
    resid_ref, dest_ref, column_ref, geometry_ref, beam_ref = buffers
    bins = resid_ref.shape[1]
    peers = send_ref.shape[0]
    dest = dest_ref[...]
    dest_f = dest.astype(F32)
    dest_t = jnp.broadcast_to(dest_f, (LANES, bins)).T
    ranks = []
    for chunk in range(bins // LANES):
        rows = (chunk + 1) * LANES
        same = dest_t[:rows] == dest_f[:, chunk * LANES : rows]
        before = iota((rows, LANES), 0) < iota((rows, LANES), 1) + chunk * LANES
        ranks.append(jnp.sum(jnp.where(same & before, 1.0, 0.0), axis=0, keepdims=True))
    rank = jnp.concatenate(ranks, axis=1)
    onehot = jnp.where(iota((peers, bins), 0) == dest, 1.0, 0.0).astype(BF16)
    for k in (0, 2, 3, 4):
        copies[k].wait()
    alive = jnp.where(iota((1, bins), 1) < live_ref[0], 1.0, 0.0)
    weighted = geometry_ref[...] * (alive * resid_ref[...])
    payload = jnp.concatenate(
        [
            beam_ref[...],
            weighted,
            column_ref[...].astype(F32),
            jnp.zeros((WIDTH - LEVELS - FIELDS - 1, bins), F32),
        ],
        axis=0,
    )
    spread = jnp.concatenate([jnp.where(rank == float(s), payload, 0.0) for s in range(SLOTS)], axis=0)
    high, low = split_two(spread)
    both = dot_nt(onehot, jnp.concatenate([high, low], axis=0))
    send_ref[...] = both[:, : SLOTS * WIDTH] + both[:, SLOTS * WIDTH :]


def coef_kernel(x_flat, y_flat, x_cols, y_cols, y_rows, mat_ref, tab_ref, edge_ref, block_ref, ends_ref, chain, gammas, betas):
    own_x = lax.axis_index("gx")
    own_y = lax.axis_index("gy")
    length = y_rows.shape[1] * LANES
    span = x_cols.shape[2] * CX

    def block_scalars(cols, row):
        steps, blocks = cols.shape[1:]

        def forward(p, value):
            value = value * cols[0, pl.ds(p, 1), :]
            gammas[pl.ds(p, 1), :blocks] = value
            return value

        alpha = lax.fori_loop(0, steps, forward, jnp.ones((1, blocks), F32))

        def backward(k, carried):
            gamma, beta = carried
            p = steps - 1 - k
            later = cols[1, pl.ds(p, 1), :]
            gamma = cols[2, pl.ds(p, 1), :] * gammas[pl.ds(p, 1), :blocks] + later * gamma
            beta = beta * later
            gammas[pl.ds(p, 1), :blocks] = gamma
            betas[pl.ds(p, 1), :blocks] = beta
            return gamma, beta

        gamma, beta = lax.fori_loop(
            0, steps, backward, (jnp.zeros((1, blocks), F32), jnp.ones((1, blocks), F32))
        )
        block_ref[row : row + 1, :blocks] = alpha
        block_ref[row + 1 : row + 2, :blocks] = beta
        block_ref[row + 2 : row + 3, :blocks] = gamma

    block_ref[...] = jnp.zeros(block_ref.shape, F32)
    block_scalars(y_cols, 3)
    block_scalars(x_cols, 0)
    blocks = x_cols.shape[2]
    mine = iota((CX, blocks), 1) == own_x
    for k, scratch in enumerate((gammas, betas)):
        picked = jnp.where(mine, scratch[:CX, :blocks] * x_cols[2], 0.0)
        ends_ref[k * CX : (k + 1) * CX] = jnp.broadcast_to(
            jnp.sum(picked, axis=1, keepdims=True), (CX, LANES)
        )

    lane = iota((1, LANES), 1)
    first = own_x * CX
    down = []
    weight = jnp.float32(1.0)
    for x in range(CX):
        down.append(weight * x_flat[2 * span + first + x])
        weight = weight * x_flat[span + first + x]
    tail, start = jnp.float32(1.0), down[CX - 1]
    tails, starts = [tail], [start]
    for x in reversed(range(CX - 1)):
        factor = x_flat[first + x + 1]
        tail = tail * factor
        start = down[x] + factor * start
        tails.append(tail)
        starts.append(start)
    row_tail = jnp.zeros((1, LANES), F32)
    row_start = jnp.zeros((1, LANES), F32)
    for x in range(CX):
        row_tail = jnp.where(lane % CX == x, tails[CX - 1 - x], row_tail)
        row_start = jnp.where(lane % CX == x, starts[CX - 1 - x], row_start)

    first = own_y * CY

    def fill(n, row):
        row = jnp.where(lane == n, 1.0, row * y_flat[first + n])
        chain[pl.ds(n, 1), :] = row
        return row

    lax.fori_loop(0, CY, fill, jnp.zeros((1, LANES), F32))

    def unfill(k, row):
        n = CY - 1 - k
        row = chain[pl.ds(n, 1), :] * y_flat[2 * length + first + n] + row * y_flat[length + first + n]
        chain[pl.ds(n, 1), :] = row
        return row

    lax.fori_loop(0, CY, unfill, jnp.zeros((1, LANES), F32))
    scale = y_rows[2, pl.ds(own_y, 1), :]
    filt = chain[...].T * scale
    high, low = split_two(filt)
    mat_ref[:CY, :CY] = high
    mat_ref[:CY, CY:] = low
    mat_ref[CY:, :CY] = high
    mat_ref[CY:, CY:] = jnp.zeros((CY, CY), BF16)
    scale_first = scale[:, :1]
    scale_last = scale[:, CY - 1 :]
    tab_ref[0] = jnp.broadcast_to(filt[:, CY - 1 :] / (scale_last * scale_last), (CY, LANES))
    tab_ref[1] = jnp.broadcast_to(filt[:, :1] / scale_first, (CY, LANES))
    edge_ref[...] = jnp.zeros(edge_ref.shape, F32)
    edge_ref[0:1] = filt[:1] * y_flat[first]
    edge_ref[1:2] = filt[CY - 1 :] * y_flat[length + first + CY - 1] / scale_last
    edge_ref[2:3] = row_tail
    edge_ref[3:4] = row_start
    for c, row in enumerate((row_tail, row_start)):
        tab_ref[2 + c] = jnp.broadcast_to(jnp.where(lane < CX, row, 0.0), (LANES, LANES)).T


def on_lines(turned, s):
    row = s * WIDTH + LEVELS + FIELDS
    place = turned[row : row + 1].astype(I32)
    on_y = iota((CY, place.shape[1]), 0) == (place & (CY - 1))
    on_x = iota((CX, place.shape[1]), 0) == (place >> 7)
    return on_x, on_y


def weighted_hits(on_line, on_cross, columns):
    rows = []
    for column in columns:
        weight = jnp.sum(jnp.where(on_cross, column, 0.0), axis=0, keepdims=True)
        rows += list(split_two(jnp.where(on_line, weight, 0.0)))
    return jnp.concatenate(rows, axis=0)


def fill_outer(turned_ref, outer):
    sources = turned_ref.shape[1]
    for s in range(SLOTS):
        at = slice(s * sources, (s + 1) * sources)
        base = s * WIDTH
        for f in range(FIELDS):
            high, low = split_two(
                turned_ref[base : base + LEVELS] * turned_ref[base + LEVELS + f : base + LEVELS + f + 1]
            )
            outer[f * LEVELS : (f + 1) * LEVELS, at] = high
            outer[DEPTH + f * LEVELS : DEPTH + (f + 1) * LEVELS, at] = low


def ends_kernel(recv_ref, sigma_ref, tab_ref, scalars, turned_out, ends_out, outer):
    sources = recv_ref.shape[0]
    turned = recv_ref[...].T
    turned_out[...] = turned
    columns = [jnp.concatenate([tab_ref[c]] * (sources // LANES), axis=1) for c in range(2)]
    hits = []
    for s in range(SLOTS):
        on_x, on_y = on_lines(turned, s)
        hits.append(weighted_hits(on_x, on_y, columns))
    fill_outer(turned_out, outer)
    summed = dot_nt(outer[...], jnp.concatenate(hits, axis=1))
    summed = (summed[:DEPTH] + summed[DEPTH:]) * sigma_ref[...]
    summed = summed + pltpu.roll(summed, LANES - CX, 1)
    own = lax.axis_index("gy")
    folded = pltpu.roll(summed, 64, 1) + scalars[pl.ds(TURN_Y + own, 1), :] * summed
    rows = DEPTH // 4
    quarter = iota((rows, LANES), 1) // CX
    fore_row, back_row = summed[:rows], folded[:rows]
    for q in range(1, 4):
        at = slice(q * rows, (q + 1) * rows)
        fore_row = jnp.where(quarter == q, pltpu.roll(summed[at], q * CX, 1), fore_row)
        back_row = jnp.where(quarter == q, pltpu.roll(folded[at], q * CX, 1), back_row)
    for j in range(ends_out.shape[0]):
        ends_out[j] = jnp.where(own <= j, fore_row, back_row)


def y_filter(values, mat_ref):
    passed = dot_nn(jnp.concatenate(split_two(values), axis=1), mat_ref[...])
    return passed[:, :CY] + passed[:, CY:]


def place_steps(begin, end, pair, outer, hit, sigma, mat_ref, masked, emit):
    def step(n, carried):
        for c in range(GROUP):
            keep = jnp.where(pair == n * GROUP + c, 1.0, 0.0)
            keep = jnp.broadcast_to(keep, (16, keep.shape[1])).astype(BF16)
            for r in range(2 * DEPTH // 16):
                masked[c * 2 * DEPTH + r * 16 : c * 2 * DEPTH + (r + 1) * 16] = (
                    outer[r * 16 : (r + 1) * 16] * keep
                )
        summed = dot_nn(masked[...], hit[...])
        parts = []
        for c in range(GROUP):
            base = c * 2 * DEPTH
            total = summed[base : base + DEPTH] + summed[base + DEPTH : base + 2 * DEPTH]
            parts += [total[:, :CY] * sigma, total[:, CY:] * sigma]
        passed = y_filter(jnp.concatenate(parts, axis=0), mat_ref)
        return emit(n, passed, carried)

    return functools.partial(lax.fori_loop, begin, end, step)


def pairs_of(turned_ref):
    rows = [turned_ref[s * WIDTH + LEVELS + FIELDS : s * WIDTH + LEVELS + FIELDS + 1] for s in range(SLOTS)]
    return jnp.concatenate(rows, axis=1).astype(I32) >> 8


def fill_hit(recv_ref, hit):
    sources = recv_ref.shape[0]
    lane2 = iota((1, 2 * LANES), 1)
    for s in range(SLOTS):
        place = s * WIDTH + LEVELS + FIELDS
        cols = jnp.broadcast_to(recv_ref[:, place : place + 1], (sources, LANES)).astype(I32) & (2 * CY - 1)
        cols = jnp.concatenate([cols, cols], axis=1)
        hit[s * sources : (s + 1) * sources] = jnp.where(cols == lane2, 1.0, 0.0).astype(BF16)


def early_kernel(turned_ref, recv_ref, sigma_ref, tab_ref, mat_ref, sums_out, block_out, masked, hit, outer):
    fill_outer(turned_ref, outer)
    turned = turned_ref[...]
    sources = turned.shape[1]
    sigma = sigma_ref[...]
    columns = [jnp.concatenate([tab_ref[2 + c, :CX]] * (sources // LANES), axis=1) for c in range(2)]
    hits = []
    for s in range(SLOTS):
        on_x, on_y = on_lines(turned, s)
        hits.append(weighted_hits(on_y, on_x, columns))
    summed = dot_nt(outer[...], jnp.concatenate(hits, axis=1))
    summed = summed[:DEPTH] + summed[DEPTH:]
    both = [(summed[:, k : k + CY] + summed[:, k + CY : k + 2 * CY]) * sigma for k in (0, 2 * CY)]
    both = y_filter(jnp.concatenate(both, axis=0), mat_ref)
    sums_out[0] = both[:DEPTH]
    sums_out[1] = both[DEPTH:]

    fill_hit(recv_ref, hit)

    def emit(n, passed, carried):
        for h in range(2 * GROUP):
            block_out[n * 2 * GROUP + h] = passed[h * DEPTH : (h + 1) * DEPTH]
        return carried

    place_steps(0, EARLY, pairs_of(turned_ref), outer, hit, sigma, mat_ref, masked, emit)(0)


def grid_kernel(x_flat, turned_ref, recv_ref, block_ref, sigma_ref, mat_ref, both_ref, edge_ref, out_ref, masked, scaled, hit, outer):
    fill_hit(recv_ref, hit)
    fill_outer(turned_ref, outer)
    first = lax.axis_index("gx") * CX
    length = x_flat.shape[0] // 3
    both = both_ref[...]
    edge_fore = edge_ref[0:1]
    edge_back = edge_ref[1:2]

    def advance(x, part, fore, back, run):
        part = part + fore * edge_fore + back * edge_back
        run = part + jnp.where(x == 0, 0.0, x_flat[first + x]) * run
        scaled[x] = x_flat[2 * length + first + x] * run
        return run

    run = jnp.zeros((DEPTH, LANES), F32)
    for x in range(EARLY * 2 * GROUP):
        run = advance(x, block_ref[x], both[:, x : x + 1], both[:, CX + x : CX + x + 1], run)

    def emit(n, passed, run):
        turn = pltpu.roll(both, lax.rem(LANES - n * 2 * GROUP, LANES), 1)
        for h in range(2 * GROUP):
            part = passed[h * DEPTH : (h + 1) * DEPTH]
            run = advance(n * 2 * GROUP + h, part, turn[:, h : h + 1], turn[:, CX + h : CX + h + 1], run)
        return run

    steps = CX // (2 * GROUP)
    place_steps(EARLY, steps, pairs_of(turned_ref), outer, hit, sigma_ref[...], mat_ref, masked, emit)(run)
    back = jnp.zeros((DEPTH, LANES), F32)
    for x in reversed(range(CX)):
        back = scaled[x] if x == CX - 1 else scaled[x] + x_flat[length + first + x] * back
        out_ref[pl.ds(x, DEPTH, stride=CX), :] = x_flat[2 * length + first + x] * back


def line_kernel(tab, ends_ref, edge_ref, raw_ref, both_out, sums_out):
    own = lax.axis_index("gy")
    count, rows, _ = ends_ref.shape
    fore = jnp.zeros((rows, LANES), F32)
    for j in range(count - 1):
        fore = jnp.where(j < own, ends_ref[j] + tab[ALPHA_Y + j : ALPHA_Y + j + 1, :] * fore, fore)
    back = jnp.zeros((rows, LANES), F32)
    for j in reversed(range(1, count)):
        back = jnp.where(j > own, ends_ref[j] + tab[BETA_Y + j : BETA_Y + j + 1, :] * back, back)
    mine = ends_ref[own] + tab[pl.ds(ALPHA_Y + own, 1), :] * fore
    back = back + tab[pl.ds(FOLD_Y + own + 1, 1), :] * mine
    lane = iota((DEPTH, LANES), 1)
    parts = []
    for q in range(4):
        left = fore if q == 0 else pltpu.roll(fore, LANES - q * CX, 1)
        right = back if q == 1 else pltpu.roll(back, (LANES - q * CX + CX) % LANES, 1)
        parts.append(jnp.where(lane[:rows] < CX, left, right))
    both = jnp.concatenate(parts, axis=0)
    both_out[...] = both
    edge_fore = edge_ref[0:1]
    edge_back = edge_ref[1:2]
    rows = DEPTH // NEAR
    for c in range(2):
        weighted = both * edge_ref[2 + c : 3 + c]
        fore_part = jnp.sum(jnp.where(lane < CX, weighted, 0.0), axis=1, keepdims=True)
        back_part = jnp.sum(jnp.where((lane >= CX) & (lane < 2 * CX), weighted, 0.0), axis=1, keepdims=True)
        total = raw_ref[c] + fore_part * edge_fore + back_part * edge_back
        for k in range(NEAR):
            sums_out[k, c * rows : (c + 1) * rows] = total[k * rows : (k + 1) * rows]


def chain_kernel(block_tab, out):
    zero, one = jnp.float32(0.0), jnp.float32(1.0)

    def put(row, value):
        out[row : row + 1, :] = jnp.full((1, LANES), value, F32)

    for i in range(NX_BLOCKS):
        put(ALPHA_X + i, block_tab[0, i])
        put(BETA_X + i, block_tab[1, i])
        put(GAMMA_X + i, block_tab[2, i])
    fold = zero
    put(FOLD_G + NX_GROUPS, fold)
    for g in reversed(range(NX_GROUPS)):
        entries = [one]
        for k in range(NEAR):
            entries.append(entries[-1] * block_tab[0, g * NEAR + k])
        gamma, beta = zero, one
        for k in reversed(range(NEAR)):
            step = block_tab[1, g * NEAR + k]
            gamma = block_tab[2, g * NEAR + k] * entries[k] + step * gamma
            beta = beta * step
        put(ALPHA_G + g, entries[NEAR])
        put(BETA_G + g, beta)
        put(TURN_G + g, beta * fold)
        fold = gamma + beta * entries[NEAR] * fold
        put(FOLD_G + g, fold)
    fold = zero
    put(FOLD_Y + NY_BLOCKS, fold)
    for j in reversed(range(NY_BLOCKS)):
        alpha, beta = block_tab[3, j], block_tab[4, j]
        put(ALPHA_Y + j, alpha)
        put(BETA_Y + j, beta)
        put(TURN_Y + j, beta * fold)
        fold = block_tab[5, j] + beta * alpha * fold
        put(FOLD_Y + j, fold)


def join_kernel(tab, sums_ref, joined_out):
    own = lax.axis_index("gx") // NEAR
    start = own * NEAR
    rows = sums_ref.shape[1] // 2
    fore = jnp.zeros((rows, LANES), F32)
    fores = []
    for k in range(NEAR):
        fores.append(fore)
        fore = sums_ref[k, :rows] + tab[pl.ds(ALPHA_X + start + k, 1), :] * fore
    back = jnp.zeros((rows, LANES), F32)
    for k in reversed(range(NEAR)):
        back = (
            sums_ref[k, rows:]
            + tab[pl.ds(GAMMA_X + start + k, 1), :] * fores[k]
            + tab[pl.ds(BETA_X + start + k, 1), :] * back
        )
    back = back + tab[pl.ds(TURN_G + own, 1), :] * fore
    for g in range(joined_out.shape[0]):
        joined_out[g] = jnp.where(own <= g, fore, back)


def carry_kernel(tab, joined_ref, sums_ref, carry_out):
    own = lax.axis_index("gx") // NEAR
    start = own * NEAR
    groups, rows, _ = joined_ref.shape
    fore = jnp.zeros((rows, LANES), F32)
    for g in range(groups - 1):
        fore = jnp.where(g < own, joined_ref[g] + tab[ALPHA_G + g : ALPHA_G + g + 1, :] * fore, fore)
    back = jnp.zeros((rows, LANES), F32)
    for g in reversed(range(1, groups)):
        back = jnp.where(g > own, joined_ref[g] + tab[BETA_G + g : BETA_G + g + 1, :] * back, back)
    mine = joined_ref[own] + tab[pl.ds(ALPHA_G + own, 1), :] * fore
    back = back + tab[pl.ds(FOLD_G + own + 1, 1), :] * mine
    fores = []
    for k in range(NEAR):
        carry_out[k, :rows] = fore
        fores.append(fore)
        fore = sums_ref[k, :rows] + tab[pl.ds(ALPHA_X + start + k, 1), :] * fore
    for k in reversed(range(NEAR)):
        carry_out[k, rows:] = back
        back = (
            sums_ref[k, rows:]
            + tab[pl.ds(GAMMA_X + start + k, 1), :] * fores[k]
            + tab[pl.ds(BETA_X + start + k, 1), :] * back
        )


def final_kernel(carry_ref, ends_ref, block_ref, out_ref):
    rows = carry_ref.shape[1] // 2
    fore = ends_ref[:CX]
    back = ends_ref[CX:]
    per = DEPTH // FINAL_STEPS
    step = pl.program_id(0)
    base = step * (per * CX)
    for r in range(per):
        if per <= rows:
            chunk, row = step * per // rows, (step * per) % rows + r
        else:
            chunk, row = step * (per // rows) + r // rows, r % rows
        out_ref[r * CX : (r + 1) * CX] = (
            block_ref[pl.ds(pl.multiple_of(base + r * CX, CX), CX), :]
            + carry_ref[chunk, pl.ds(row, 1), :] * fore
            + carry_ref[chunk, pl.ds(rows + row, 1), :] * back
        )


def table(gap):
    decay = 1.0 - gap
    edge = jnp.zeros((1,), F32)
    prior = jnp.concatenate([edge, decay[:-1]])
    later = jnp.concatenate([decay[1:], edge])
    return jnp.stack([prior, later, jnp.sqrt(gap * (2.0 - gap))])


def call(kernel, outs, specs, scratch=(), mib=48):
    shapes = tuple(jax.ShapeDtypeStruct(s, t) for s, t in outs)
    return pl.pallas_call(
        kernel,
        out_shape=shapes if len(shapes) > 1 else shapes[0],
        in_specs=specs,
        out_specs=(vmem,) * len(shapes) if len(shapes) > 1 else vmem,
        scratch_shapes=scratch,
        compiler_params=params(mib),
    )


def local(bin_resid, geometry, beam_weight, dest_device, dest_column, live_count, field_sigma, x_gap, y_gap):
    count_x = lax.axis_size("gx")
    count_y = lax.axis_size("gy")
    peers = count_x * count_y
    bins = bin_resid.shape[0]
    slots = SLOTS * peers
    far = count_x // NEAR
    chunk = 2 * DEPTH // NEAR
    near_groups = [[g * NEAR + k for k in range(NEAR)] for g in range(far)]
    far_groups = [[g * NEAR + k for g in range(far)] for k in range(NEAR)]
    side_groups = [[i * count_y + j for i in group for j in range(count_y)] for group in near_groups]
    a2a = functools.partial(lax.all_to_all, tiled=True)
    tie = lax.optimization_barrier

    row = (1, bins)
    moved = call(
        pack_kernel,
        [((peers, SLOTS * WIDTH), F32)],
        [smem] + [hbm] * 5,
        [
            pltpu.VMEM(row, F32),
            pltpu.VMEM(row, I32),
            pltpu.VMEM(row, I32),
            pltpu.VMEM((FIELDS, bins), F32),
            pltpu.VMEM((LEVELS, bins), F32),
            pltpu.SemaphoreType.DMA((5,)),
        ],
        60,
    )(
        live_count,
        bin_resid.reshape(row),
        dest_device.reshape(row),
        dest_column.reshape(row),
        geometry,
        beam_weight,
    )
    tab_x = table(x_gap)
    tab_y = table(y_gap)
    x_flat = tab_x.reshape(-1)
    sigma = jnp.broadcast_to(field_sigma.reshape(DEPTH, 1), (DEPTH, LANES))
    coefs = call(
        coef_kernel,
        [
            ((2 * CY, 2 * CY), BF16),
            ((4, CY, LANES), F32),
            ((8, LANES), F32),
            ((8, LANES), F32),
            ((2 * CX, LANES), F32),
        ],
        [smem, smem, vmem, vmem, vmem],
        [pltpu.VMEM((CY, LANES), F32)] * 3,
    )(
        x_flat,
        tab_y.reshape(-1),
        tab_x.reshape(3, count_x, CX).transpose(0, 2, 1),
        tab_y.reshape(3, count_y, CY).transpose(0, 2, 1),
        tab_y.reshape(3, count_y, CY),
    )
    scalars = call(chain_kernel, [((TAB_ROWS, LANES), F32)], [smem])(coefs[3])
    mat, tab, edge, _, x_ends = coefs
    moved = a2a(moved.reshape(peers, 1, SLOTS * WIDTH), ("gx", "gy"), split_axis=0, concat_axis=0)
    moved, coefs, sigma, scalars = tie((moved, coefs, sigma, scalars))
    moved = moved.reshape(peers, SLOTS * WIDTH)
    outer = pltpu.VMEM((2 * DEPTH, slots), BF16)
    hit = pltpu.VMEM((slots, 2 * CY), BF16)
    turned, ends = call(
        ends_kernel,
        [((SLOTS * WIDTH, peers), F32), ((count_y, DEPTH // 4, LANES), F32)],
        [vmem] * 4,
        [outer],
    )(moved, sigma, tab, scalars)
    ends = a2a(ends, "gy", split_axis=0, concat_axis=0)
    masked = pltpu.VMEM((GROUP * 2 * DEPTH, slots), BF16)
    raw, block = call(
        early_kernel,
        [
            ((2, DEPTH, LANES), F32),
            ((EARLY * 2 * GROUP, DEPTH, LANES), F32),
        ],
        [vmem] * 5,
        [masked, hit, outer],
    )(turned, moved, sigma, tab, mat)
    both, sums = call(
        line_kernel,
        [((DEPTH, LANES), F32), ((NEAR, chunk, LANES), F32)],
        [vmem] * 4,
    )(scalars, ends, edge, raw)
    sums = a2a(sums, "gx", split_axis=0, concat_axis=0, axis_index_groups=near_groups)
    joined = call(join_kernel, [((far, chunk // 2, LANES), F32)], [vmem, vmem])(scalars, sums)
    joined, both = tie((joined, both))
    joined = a2a(joined, "gx", split_axis=0, concat_axis=0, axis_index_groups=far_groups)
    block = call(
        grid_kernel,
        [((DEPTH * CX, LANES), F32)],
        [smem] + [vmem] * 7,
        [masked, pltpu.VMEM((CX, DEPTH, LANES), F32), hit, outer],
    )(x_flat, turned, moved, block, sigma, mat, both, edge)
    joined, block = tie((joined, block))
    carry = call(carry_kernel, [((NEAR, chunk, LANES), F32)], [vmem] * 3)(scalars, joined, sums)
    carry = a2a(carry, "gx", split_axis=0, concat_axis=0, axis_index_groups=near_groups)
    rows = DEPTH * CX // FINAL_STEPS
    out = pl.pallas_call(
        final_kernel,
        grid=(FINAL_STEPS,),
        out_shape=jax.ShapeDtypeStruct((DEPTH * CX, LANES), F32),
        in_specs=[vmem] * 3,
        out_specs=pl.BlockSpec((rows, LANES), lambda k: (k, 0)),
        compiler_params=params(),
    )(carry, x_ends, block)
    return out.reshape(FIELDS, LEVELS, CX, CY)


def solution(mesh):
    both = ("gx", "gy")
    placed = (P(both), P(None, both), P(None, both), P(both, None), P(both), P(both), P(), P(), P())
    return jax.shard_map(
        local, mesh=mesh, in_specs=placed, out_specs=P(None, None, "gx", "gy"), check_vma=False
    )
```

```python
import functools
import jax
import jax.numpy as jnp
from jax import lax
from jax.experimental import pallas as pl
from jax.experimental.pallas import tpu as pltpu
from jax.sharding import PartitionSpec as P

F32 = jnp.float32
BF16 = jnp.bfloat16
I32 = jnp.int32
LANES = 128
FIELDS = 6
LEVELS = 16
DEPTH = FIELDS * LEVELS
SLOTS = 4
WIDTH = 24
CX = 32
CY = 128
NEAR = 4
GROUP = 4
SPREAD, UNSPREAD = 37, 429
FINAL_STEPS = 2
EARLY = 1
NX_GROUPS = 8
NX_BLOCKS = NX_GROUPS * NEAR
NY_BLOCKS = 16
ALPHA_X, BETA_X, GAMMA_X = 0, 32, 64
ALPHA_Y, BETA_Y, FOLD_Y, TURN_Y = 96, 112, 128, 152
ALPHA_G, BETA_G, FOLD_G, TURN_G = 168, 176, 184, 200
TAB_ROWS = 208


def params(mib=48):
    return pltpu.CompilerParams(vmem_limit_bytes=mib * 1024 * 1024)


vmem = pl.BlockSpec(memory_space=pltpu.VMEM)
smem = pl.BlockSpec(memory_space=pltpu.SMEM)
hbm = pl.BlockSpec(memory_space=pltpu.HBM)


def iota(shape, dim):
    return lax.broadcasted_iota(I32, shape, dim)


def split_two(values):
    high = values.astype(BF16)
    return high, (values - high.astype(F32)).astype(BF16)


def dot_nt(left, right):
    return lax.dot_general(left, right, (((1,), (1,)), ((), ())), preferred_element_type=F32)


def dot_nn(left, right):
    return lax.dot_general(left, right, (((1,), (0,)), ((), ())), preferred_element_type=F32)


def pack_kernel(live_ref, *refs):
    sources, (send_ref, *buffers, sems) = refs[:5], refs[5:]
    copies = [pltpu.make_async_copy(src, buf, sems.at[k]) for k, (src, buf) in enumerate(zip(sources, buffers))]
    for k in (1, 0, 2, 3, 4):
        copies[k].start()
    copies[1].wait()
    resid_ref, dest_ref, column_ref, geometry_ref, beam_ref = buffers
    bins = resid_ref.shape[1]
    peers = send_ref.shape[0]
    dest = dest_ref[...]
    dest_f = dest.astype(F32)
    dest_t = jnp.broadcast_to(dest_f, (LANES, bins)).T
    ranks = []
    for chunk in range(bins // LANES):
        rows = (chunk + 1) * LANES
        same = dest_t[:rows] == dest_f[:, chunk * LANES : rows]
        before = iota((rows, LANES), 0) < iota((rows, LANES), 1) + chunk * LANES
        ranks.append(jnp.sum(jnp.where(same & before, 1.0, 0.0), axis=0, keepdims=True))
    rank = jnp.concatenate(ranks, axis=1)
    place = (dest * UNSPREAD) & (peers - 1)
    onehot = jnp.where(iota((peers, bins), 0) == place, 1.0, 0.0).astype(BF16)
    for k in (0, 2, 3, 4):
        copies[k].wait()
    alive = jnp.where(iota((1, bins), 1) < live_ref[0], 1.0, 0.0)
    weighted = geometry_ref[...] * (alive * resid_ref[...])
    payload = jnp.concatenate(
        [
            beam_ref[...],
            weighted,
            column_ref[...].astype(F32),
            jnp.zeros((WIDTH - LEVELS - FIELDS - 1, bins), F32),
        ],
        axis=0,
    )
    spread = jnp.concatenate([jnp.where(rank == float(s), payload, 0.0) for s in range(SLOTS)], axis=0)
    high, low = split_two(spread)
    both = dot_nt(onehot, jnp.concatenate([high, low], axis=0))
    send_ref[...] = both[:, : SLOTS * WIDTH] + both[:, SLOTS * WIDTH :]


def coef_kernel(x_flat, y_flat, x_cols, y_cols, y_rows, mat_ref, tab_ref, edge_ref, block_ref, ends_ref, chain, entry):
    own_x = lax.axis_index("gx")
    own_y = lax.axis_index("gy")
    length = y_rows.shape[1] * LANES
    span = x_cols.shape[2] * CX

    block_ref[...] = jnp.zeros(block_ref.shape, F32)
    blocks = x_cols.shape[2]
    alpha = jnp.ones((1, blocks), F32)
    entries = []
    for p in range(CX):
        alpha = alpha * x_cols[0, p : p + 1, :]
        entries.append(alpha)
    gamma, beta = jnp.zeros((1, blocks), F32), jnp.ones((1, blocks), F32)
    gammas, betas = [], []
    for p in reversed(range(CX)):
        later = x_cols[1, p : p + 1, :]
        gamma = x_cols[2, p : p + 1, :] * entries[p] + later * gamma
        beta = beta * later
        gammas.append(gamma)
        betas.append(beta)
    for row, value in enumerate((alpha, beta, gamma)):
        block_ref[row : row + 1, :blocks] = value
    mine = iota((CX, blocks), 1) == own_x
    for k, rows in enumerate((gammas, betas)):
        picked = jnp.where(mine, jnp.concatenate(rows[::-1], axis=0) * x_cols[2], 0.0)
        ends_ref[k * CX : (k + 1) * CX] = jnp.broadcast_to(
            jnp.sum(picked, axis=1, keepdims=True), (CX, LANES)
        )

    lane = iota((1, LANES), 1)
    first = own_x * CX
    down = []
    weight = jnp.float32(1.0)
    for x in range(CX):
        down.append(weight * x_flat[2 * span + first + x])
        weight = weight * x_flat[span + first + x]
    tail, start = jnp.float32(1.0), down[CX - 1]
    tails, starts = [tail], [start]
    for x in reversed(range(CX - 1)):
        factor = x_flat[first + x + 1]
        tail = tail * factor
        start = down[x] + factor * start
        tails.append(tail)
        starts.append(start)
    row_tail = jnp.zeros((1, LANES), F32)
    row_start = jnp.zeros((1, LANES), F32)
    for x in range(CX):
        row_tail = jnp.where(lane % CX == x, tails[CX - 1 - x], row_tail)
        row_start = jnp.where(lane % CX == x, starts[CX - 1 - x], row_start)

    first = own_y * CY
    blocks = y_cols.shape[2]
    unroll = 8

    def forward(k, carried):
        alpha, row = carried
        for u in range(unroll):
            n = k * unroll + u
            alpha = alpha * y_cols[0, pl.ds(n, 1), :]
            entry[pl.ds(n, 1), :blocks] = alpha
            row = jnp.where(lane == n, 1.0, row * y_flat[first + n])
            chain[pl.ds(n, 1), :] = row
        return alpha, row

    none = jnp.zeros((1, LANES), F32)
    one = jnp.ones((1, blocks), F32)
    alpha, _ = lax.fori_loop(0, CY // unroll, forward, (one, none))

    def backward(k, carried):
        gamma, beta, row = carried
        for u in range(unroll):
            n = CY - 1 - (k * unroll + u)
            later = y_cols[1, pl.ds(n, 1), :]
            gamma = y_cols[2, pl.ds(n, 1), :] * entry[pl.ds(n, 1), :blocks] + later * gamma
            beta = beta * later
            row = chain[pl.ds(n, 1), :] * y_flat[2 * length + first + n] + row * y_flat[length + first + n]
            chain[pl.ds(n, 1), :] = row
        return gamma, beta, row

    gamma, beta, _ = lax.fori_loop(0, CY // unroll, backward, (jnp.zeros((1, blocks), F32), one, none))
    for row, value in enumerate((alpha, beta, gamma)):
        block_ref[3 + row : 4 + row, :blocks] = value
    scale = y_rows[2, pl.ds(own_y, 1), :]
    filt = chain[...].T * scale
    high, low = split_two(filt)
    mat_ref[:CY, :CY] = high
    mat_ref[:CY, CY:] = low
    mat_ref[CY:, :CY] = high
    mat_ref[CY:, CY:] = jnp.zeros((CY, CY), BF16)
    scale_first = scale[:, :1]
    scale_last = scale[:, CY - 1 :]
    tab_ref[0] = jnp.broadcast_to(filt[:, CY - 1 :] / (scale_last * scale_last), (CY, LANES))
    tab_ref[1] = jnp.broadcast_to(filt[:, :1] / scale_first, (CY, LANES))
    edge_ref[...] = jnp.zeros(edge_ref.shape, F32)
    edge_ref[0:1] = filt[:1] * y_flat[first]
    edge_ref[1:2] = filt[CY - 1 :] * y_flat[length + first + CY - 1] / scale_last
    edge_ref[2:3] = row_tail
    edge_ref[3:4] = row_start
    for c, row in enumerate((row_tail, row_start)):
        tab_ref[2 + c] = jnp.broadcast_to(jnp.where(lane < CX, row, 0.0), (LANES, LANES)).T


def on_lines(turned, s):
    row = s * WIDTH + LEVELS + FIELDS
    place = turned[row : row + 1].astype(I32)
    on_y = iota((CY, place.shape[1]), 0) == (place & (CY - 1))
    on_x = iota((CX, place.shape[1]), 0) == (place >> 7)
    return on_x, on_y


def weighted_hits(on_line, on_cross, columns):
    rows = []
    for column in columns:
        weight = jnp.sum(jnp.where(on_cross, column, 0.0), axis=0, keepdims=True)
        rows += list(split_two(jnp.where(on_line, weight, 0.0)))
    return jnp.concatenate(rows, axis=0)


def fill_outer(turned_ref, outer):
    sources = turned_ref.shape[1]
    for s in range(SLOTS):
        at = slice(s * sources, (s + 1) * sources)
        base = s * WIDTH
        for f in range(FIELDS):
            high, low = split_two(
                turned_ref[base : base + LEVELS] * turned_ref[base + LEVELS + f : base + LEVELS + f + 1]
            )
            outer[f * LEVELS : (f + 1) * LEVELS, at] = high
            outer[DEPTH + f * LEVELS : DEPTH + (f + 1) * LEVELS, at] = low


def ends_kernel(recv_ref, sigma_ref, tab_ref, scalars, turned_out, ends_out, outer):
    sources = recv_ref.shape[0]
    turned = recv_ref[...].T
    turned_out[...] = turned
    columns = [jnp.concatenate([tab_ref[c]] * (sources // LANES), axis=1) for c in range(2)]
    hits = []
    for s in range(SLOTS):
        on_x, on_y = on_lines(turned, s)
        hits.append(weighted_hits(on_x, on_y, columns))
    fill_outer(turned_out, outer)
    summed = dot_nt(outer[...], jnp.concatenate(hits, axis=1))
    summed = (summed[:DEPTH] + summed[DEPTH:]) * sigma_ref[...]
    summed = summed + pltpu.roll(summed, LANES - CX, 1)
    own = lax.axis_index("gy")
    folded = pltpu.roll(summed, 64, 1) + scalars[pl.ds(TURN_Y + own, 1), :] * summed
    rows = DEPTH // 4
    quarter = iota((rows, LANES), 1) // CX
    fore_row, back_row = summed[:rows], folded[:rows]
    for q in range(1, 4):
        at = slice(q * rows, (q + 1) * rows)
        fore_row = jnp.where(quarter == q, pltpu.roll(summed[at], q * CX, 1), fore_row)
        back_row = jnp.where(quarter == q, pltpu.roll(folded[at], q * CX, 1), back_row)
    for j in range(ends_out.shape[0]):
        ends_out[j] = jnp.where(own <= j, fore_row, back_row)


def y_filter(values, mat_ref):
    passed = dot_nn(jnp.concatenate(split_two(values), axis=1), mat_ref[...])
    return passed[:, :CY] + passed[:, CY:]


def place_steps(begin, end, pair, outer, hit, sigma, mat_ref, masked, emit):
    def step(n, carried):
        for c in range(GROUP):
            keep = jnp.where(pair == n * GROUP + c, 1.0, 0.0)
            keep = jnp.broadcast_to(keep, (16, keep.shape[1])).astype(BF16)
            for r in range(2 * DEPTH // 16):
                masked[c * 2 * DEPTH + r * 16 : c * 2 * DEPTH + (r + 1) * 16] = (
                    outer[r * 16 : (r + 1) * 16] * keep
                )
        summed = dot_nn(masked[...], hit[...])
        parts = []
        for c in range(GROUP):
            base = c * 2 * DEPTH
            total = summed[base : base + DEPTH] + summed[base + DEPTH : base + 2 * DEPTH]
            parts += [total[:, :CY] * sigma, total[:, CY:] * sigma]
        passed = y_filter(jnp.concatenate(parts, axis=0), mat_ref)
        return emit(n, passed, carried)

    return functools.partial(lax.fori_loop, begin, end, step)


def pairs_of(turned_ref):
    rows = [turned_ref[s * WIDTH + LEVELS + FIELDS : s * WIDTH + LEVELS + FIELDS + 1] for s in range(SLOTS)]
    return jnp.concatenate(rows, axis=1).astype(I32) >> 8


def fill_hit(recv_ref, hit):
    sources = recv_ref.shape[0]
    lane2 = iota((1, 2 * LANES), 1)
    for s in range(SLOTS):
        place = s * WIDTH + LEVELS + FIELDS
        cols = jnp.broadcast_to(recv_ref[:, place : place + 1], (sources, LANES)).astype(I32) & (2 * CY - 1)
        cols = jnp.concatenate([cols, cols], axis=1)
        hit[s * sources : (s + 1) * sources] = jnp.where(cols == lane2, 1.0, 0.0).astype(BF16)


def early_kernel(turned_ref, recv_ref, sigma_ref, tab_ref, mat_ref, sums_out, block_out, masked, hit, outer):
    fill_outer(turned_ref, outer)
    turned = turned_ref[...]
    sources = turned.shape[1]
    sigma = sigma_ref[...]
    columns = [jnp.concatenate([tab_ref[2 + c, :CX]] * (sources // LANES), axis=1) for c in range(2)]
    hits = []
    for s in range(SLOTS):
        on_x, on_y = on_lines(turned, s)
        hits.append(weighted_hits(on_y, on_x, columns))
    summed = dot_nt(outer[...], jnp.concatenate(hits, axis=1))
    summed = summed[:DEPTH] + summed[DEPTH:]
    both = [(summed[:, k : k + CY] + summed[:, k + CY : k + 2 * CY]) * sigma for k in (0, 2 * CY)]
    both = y_filter(jnp.concatenate(both, axis=0), mat_ref)
    sums_out[0] = both[:DEPTH]
    sums_out[1] = both[DEPTH:]

    fill_hit(recv_ref, hit)

    def emit(n, passed, carried):
        for h in range(2 * GROUP):
            block_out[n * 2 * GROUP + h] = passed[h * DEPTH : (h + 1) * DEPTH]
        return carried

    place_steps(0, EARLY, pairs_of(turned_ref), outer, hit, sigma, mat_ref, masked, emit)(0)


def grid_kernel(x_flat, turned_ref, recv_ref, block_ref, sigma_ref, mat_ref, both_ref, edge_ref, out_ref, masked, scaled, hit, outer):
    fill_hit(recv_ref, hit)
    fill_outer(turned_ref, outer)
    first = lax.axis_index("gx") * CX
    length = x_flat.shape[0] // 3
    both = both_ref[...]
    edge_fore = edge_ref[0:1]
    edge_back = edge_ref[1:2]

    def advance(x, part, fore, back, run):
        part = part + fore * edge_fore + back * edge_back
        run = part + jnp.where(x == 0, 0.0, x_flat[first + x]) * run
        scaled[x] = x_flat[2 * length + first + x] * run
        return run

    run = jnp.zeros((DEPTH, LANES), F32)
    for x in range(EARLY * 2 * GROUP):
        run = advance(x, block_ref[x], both[:, x : x + 1], both[:, CX + x : CX + x + 1], run)

    def emit(n, passed, run):
        turn = pltpu.roll(both, lax.rem(LANES - n * 2 * GROUP, LANES), 1)
        for h in range(2 * GROUP):
            part = passed[h * DEPTH : (h + 1) * DEPTH]
            run = advance(n * 2 * GROUP + h, part, turn[:, h : h + 1], turn[:, CX + h : CX + h + 1], run)
        return run

    steps = CX // (2 * GROUP)
    place_steps(EARLY, steps, pairs_of(turned_ref), outer, hit, sigma_ref[...], mat_ref, masked, emit)(run)
    back = jnp.zeros((DEPTH, LANES), F32)
    for x in reversed(range(CX)):
        back = scaled[x] if x == CX - 1 else scaled[x] + x_flat[length + first + x] * back
        out_ref[pl.ds(x, DEPTH, stride=CX), :] = x_flat[2 * length + first + x] * back


def line_kernel(tab, ends_ref, edge_ref, raw_ref, both_out, sums_out):
    own = lax.axis_index("gy")
    count, rows, _ = ends_ref.shape
    fore = jnp.zeros((rows, LANES), F32)
    for j in range(count - 1):
        fore = jnp.where(j < own, ends_ref[j] + tab[ALPHA_Y + j : ALPHA_Y + j + 1, :] * fore, fore)
    back = jnp.zeros((rows, LANES), F32)
    for j in reversed(range(1, count)):
        back = jnp.where(j > own, ends_ref[j] + tab[BETA_Y + j : BETA_Y + j + 1, :] * back, back)
    mine = ends_ref[own] + tab[pl.ds(ALPHA_Y + own, 1), :] * fore
    back = back + tab[pl.ds(FOLD_Y + own + 1, 1), :] * mine
    lane = iota((DEPTH, LANES), 1)
    parts = []
    for q in range(4):
        left = fore if q == 0 else pltpu.roll(fore, LANES - q * CX, 1)
        right = back if q == 1 else pltpu.roll(back, (LANES - q * CX + CX) % LANES, 1)
        parts.append(jnp.where(lane[:rows] < CX, left, right))
    both = jnp.concatenate(parts, axis=0)
    both_out[...] = both
    edge_fore = edge_ref[0:1]
    edge_back = edge_ref[1:2]
    rows = DEPTH // NEAR
    for c in range(2):
        weighted = both * edge_ref[2 + c : 3 + c]
        fore_part = jnp.sum(jnp.where(lane < CX, weighted, 0.0), axis=1, keepdims=True)
        back_part = jnp.sum(jnp.where((lane >= CX) & (lane < 2 * CX), weighted, 0.0), axis=1, keepdims=True)
        total = raw_ref[c] + fore_part * edge_fore + back_part * edge_back
        for k in range(NEAR):
            sums_out[k, c * rows : (c + 1) * rows] = total[k * rows : (k + 1) * rows]


def chain_kernel(block_tab, out):
    zero, one = jnp.float32(0.0), jnp.float32(1.0)

    def put(row, value):
        out[row : row + 1, :] = jnp.full((1, LANES), value, F32)

    for i in range(NX_BLOCKS):
        put(ALPHA_X + i, block_tab[0, i])
        put(BETA_X + i, block_tab[1, i])
        put(GAMMA_X + i, block_tab[2, i])
    fold = zero
    put(FOLD_G + NX_GROUPS, fold)
    for g in reversed(range(NX_GROUPS)):
        entries = [one]
        for k in range(NEAR):
            entries.append(entries[-1] * block_tab[0, g * NEAR + k])
        gamma, beta = zero, one
        for k in reversed(range(NEAR)):
            step = block_tab[1, g * NEAR + k]
            gamma = block_tab[2, g * NEAR + k] * entries[k] + step * gamma
            beta = beta * step
        put(ALPHA_G + g, entries[NEAR])
        put(BETA_G + g, beta)
        put(TURN_G + g, beta * fold)
        fold = gamma + beta * entries[NEAR] * fold
        put(FOLD_G + g, fold)
    fold = zero
    put(FOLD_Y + NY_BLOCKS, fold)
    for j in reversed(range(NY_BLOCKS)):
        alpha, beta = block_tab[3, j], block_tab[4, j]
        put(ALPHA_Y + j, alpha)
        put(BETA_Y + j, beta)
        put(TURN_Y + j, beta * fold)
        fold = block_tab[5, j] + beta * alpha * fold
        put(FOLD_Y + j, fold)


def join_kernel(tab, sums_ref, joined_out):
    own = lax.axis_index("gx") // NEAR
    start = own * NEAR
    rows = sums_ref.shape[1] // 2
    fore = jnp.zeros((rows, LANES), F32)
    fores = []
    for k in range(NEAR):
        fores.append(fore)
        fore = sums_ref[k, :rows] + tab[pl.ds(ALPHA_X + start + k, 1), :] * fore
    back = jnp.zeros((rows, LANES), F32)
    for k in reversed(range(NEAR)):
        back = (
            sums_ref[k, rows:]
            + tab[pl.ds(GAMMA_X + start + k, 1), :] * fores[k]
            + tab[pl.ds(BETA_X + start + k, 1), :] * back
        )
    back = back + tab[pl.ds(TURN_G + own, 1), :] * fore
    for g in range(joined_out.shape[0]):
        joined_out[g] = jnp.where(own <= g, fore, back)


def carry_kernel(tab, joined_ref, sums_ref, carry_out):
    own = lax.axis_index("gx") // NEAR
    start = own * NEAR
    groups, rows, _ = joined_ref.shape
    fore = jnp.zeros((rows, LANES), F32)
    for g in range(groups - 1):
        fore = jnp.where(g < own, joined_ref[g] + tab[ALPHA_G + g : ALPHA_G + g + 1, :] * fore, fore)
    back = jnp.zeros((rows, LANES), F32)
    for g in reversed(range(1, groups)):
        back = jnp.where(g > own, joined_ref[g] + tab[BETA_G + g : BETA_G + g + 1, :] * back, back)
    mine = joined_ref[own] + tab[pl.ds(ALPHA_G + own, 1), :] * fore
    back = back + tab[pl.ds(FOLD_G + own + 1, 1), :] * mine
    fores = []
    for k in range(NEAR):
        carry_out[k, :rows] = fore
        fores.append(fore)
        fore = sums_ref[k, :rows] + tab[pl.ds(ALPHA_X + start + k, 1), :] * fore
    for k in reversed(range(NEAR)):
        carry_out[k, rows:] = back
        back = (
            sums_ref[k, rows:]
            + tab[pl.ds(GAMMA_X + start + k, 1), :] * fores[k]
            + tab[pl.ds(BETA_X + start + k, 1), :] * back
        )


def final_kernel(carry_ref, ends_ref, block_ref, out_ref):
    rows = carry_ref.shape[1] // 2
    fore = ends_ref[:CX]
    back = ends_ref[CX:]
    per = DEPTH // FINAL_STEPS
    step = pl.program_id(0)
    base = step * (per * CX)
    for r in range(per):
        if per <= rows:
            chunk, row = step * per // rows, (step * per) % rows + r
        else:
            chunk, row = step * (per // rows) + r // rows, r % rows
        out_ref[r * CX : (r + 1) * CX] = (
            block_ref[pl.ds(pl.multiple_of(base + r * CX, CX), CX), :]
            + carry_ref[chunk, pl.ds(row, 1), :] * fore
            + carry_ref[chunk, pl.ds(rows + row, 1), :] * back
        )


def table(gap):
    decay = 1.0 - gap
    edge = jnp.zeros((1,), F32)
    prior = jnp.concatenate([edge, decay[:-1]])
    later = jnp.concatenate([decay[1:], edge])
    return jnp.stack([prior, later, jnp.sqrt(gap * (2.0 - gap))])


def call(kernel, outs, specs, scratch=(), mib=48):
    shapes = tuple(jax.ShapeDtypeStruct(s, t) for s, t in outs)
    return pl.pallas_call(
        kernel,
        out_shape=shapes if len(shapes) > 1 else shapes[0],
        in_specs=specs,
        out_specs=(vmem,) * len(shapes) if len(shapes) > 1 else vmem,
        scratch_shapes=scratch,
        compiler_params=params(mib),
    )


def local(bin_resid, geometry, beam_weight, dest_device, dest_column, live_count, field_sigma, x_gap, y_gap):
    count_x = lax.axis_size("gx")
    count_y = lax.axis_size("gy")
    peers = count_x * count_y
    bins = bin_resid.shape[0]
    slots = SLOTS * peers
    far = count_x // NEAR
    chunk = 2 * DEPTH // NEAR
    near_groups = [[g * NEAR + k for k in range(NEAR)] for g in range(far)]
    far_groups = [[g * NEAR + k for g in range(far)] for k in range(NEAR)]
    side_groups = [[i * count_y + j for i in group for j in range(count_y)] for group in near_groups]
    a2a = functools.partial(lax.all_to_all, tiled=True)
    tie = lax.optimization_barrier

    row = (1, bins)
    moved = call(
        pack_kernel,
        [((peers, SLOTS * WIDTH), F32)],
        [smem] + [hbm] * 5,
        [
            pltpu.VMEM(row, F32),
            pltpu.VMEM(row, I32),
            pltpu.VMEM(row, I32),
            pltpu.VMEM((FIELDS, bins), F32),
            pltpu.VMEM((LEVELS, bins), F32),
            pltpu.SemaphoreType.DMA((5,)),
        ],
        60,
    )(
        live_count,
        bin_resid.reshape(row),
        dest_device.reshape(row),
        dest_column.reshape(row),
        geometry,
        beam_weight,
    )
    tab_x = table(x_gap)
    tab_y = table(y_gap)
    x_flat = tab_x.reshape(-1)
    sigma = jnp.broadcast_to(field_sigma.reshape(DEPTH, 1), (DEPTH, LANES))
    coefs = call(
        coef_kernel,
        [
            ((2 * CY, 2 * CY), BF16),
            ((4, CY, LANES), F32),
            ((8, LANES), F32),
            ((8, LANES), F32),
            ((2 * CX, LANES), F32),
        ],
        [smem, smem, vmem, vmem, vmem],
        [pltpu.VMEM((CY, LANES), F32)] * 2,
    )(
        x_flat,
        tab_y.reshape(-1),
        tab_x.reshape(3, count_x, CX).transpose(0, 2, 1),
        tab_y.reshape(3, count_y, CY).transpose(0, 2, 1),
        tab_y.reshape(3, count_y, CY),
    )
    scalars = call(chain_kernel, [((TAB_ROWS, LANES), F32)], [smem])(coefs[3])
    mat, tab, edge, _, x_ends = coefs
    order = [[(p * SPREAD) % peers for p in range(peers)]]
    moved = a2a(
        moved.reshape(peers, 1, SLOTS * WIDTH), ("gx", "gy"), split_axis=0, concat_axis=0, axis_index_groups=order
    )
    moved, coefs, sigma, scalars = tie((moved, coefs, sigma, scalars))
    moved = moved.reshape(peers, SLOTS * WIDTH)
    outer = pltpu.VMEM((2 * DEPTH, slots), BF16)
    hit = pltpu.VMEM((slots, 2 * CY), BF16)
    turned, ends = call(
        ends_kernel,
        [((SLOTS * WIDTH, peers), F32), ((count_y, DEPTH // 4, LANES), F32)],
        [vmem] * 4,
        [outer],
    )(moved, sigma, tab, scalars)
    ends = a2a(ends, "gy", split_axis=0, concat_axis=0)
    masked = pltpu.VMEM((GROUP * 2 * DEPTH, slots), BF16)
    raw, block = call(
        early_kernel,
        [
            ((2, DEPTH, LANES), F32),
            ((EARLY * 2 * GROUP, DEPTH, LANES), F32),
        ],
        [vmem] * 5,
        [masked, hit, outer],
    )(turned, moved, sigma, tab, mat)
    both, sums = call(
        line_kernel,
        [((DEPTH, LANES), F32), ((NEAR, chunk, LANES), F32)],
        [vmem] * 4,
    )(scalars, ends, edge, raw)
    sums = a2a(sums, "gx", split_axis=0, concat_axis=0, axis_index_groups=near_groups)
    joined = call(join_kernel, [((far, chunk // 2, LANES), F32)], [vmem, vmem])(scalars, sums)
    joined, both = tie((joined, both))
    joined = a2a(joined, "gx", split_axis=0, concat_axis=0, axis_index_groups=far_groups)
    block = call(
        grid_kernel,
        [((DEPTH * CX, LANES), F32)],
        [smem] + [vmem] * 7,
        [masked, pltpu.VMEM((CX, DEPTH, LANES), F32), hit, outer],
    )(x_flat, turned, moved, block, sigma, mat, both, edge)
    joined, block = tie((joined, block))
    carry = call(carry_kernel, [((NEAR, chunk, LANES), F32)], [vmem] * 3)(scalars, joined, sums)
    carry = a2a(carry, "gx", split_axis=0, concat_axis=0, axis_index_groups=near_groups)
    rows = DEPTH * CX // FINAL_STEPS
    out = pl.pallas_call(
        final_kernel,
        grid=(FINAL_STEPS,),
        out_shape=jax.ShapeDtypeStruct((DEPTH * CX, LANES), F32),
        in_specs=[vmem] * 3,
        out_specs=pl.BlockSpec((rows, LANES), lambda k: (k, 0)),
        compiler_params=params(),
    )(carry, x_ends, block)
    return out.reshape(FIELDS, LEVELS, CX, CY)


def solution(mesh):
    both = ("gx", "gy")
    placed = (P(both), P(None, both), P(None, both), P(both, None), P(both), P(both), P(), P(), P())
    return jax.shard_map(
        local, mesh=mesh, in_specs=placed, out_specs=P(None, None, "gx", "gy"), check_vma=False
    )
```
